256 devices in a mesh: row: 8 (over z), col: 32 (over y, x, core).
Axes of the slice: x: 4, y: 4, z: 8, core: 2. Of those that a mesh axis runs over, the one named last changes fastest.
Arguments:
- weight: float32 [16384, 28672], P('row', 'col')
- sketch: bfloat16 [28672, 256], P('col')
Outputs:
- residual: bfloat16 [16384, 28672], P('row', 'col')
- left_adapter: bfloat16 [16384, 256], P('row')
- right_adapter: bfloat16 [256, 28672], P(None, 'col')
All inputs are finite; a program needn't handle non-finite values.
Results may differ from the reference program's by a relative error of at most 0.0015.
Values sent between devices are 32-bit elements; how exact they have to be, the bound alone decides.
No kernel may reach another device: no remote copies, remote signals or barrier semaphores. Data moves between devices by JAX's collectives and lax.ppermute only.
A program may use at most 64 MiB of HBM per device.

```python
import math
import jax
import jax.numpy as jnp
from jax import lax

ROWS = 16384
FFW = 28672
RANK = 256


def shared_basis(key):
    return jnp.clip(jax.random.normal(key, (FFW, RANK), jnp.float32), -5.0, 5.0)


def draw_weight(key, part):
    basis = shared_basis(key)
    key = jax.random.fold_in(key, 7)
    key_left, key_scale, key_noise = jax.random.split(key, 3)
    left_factor = jnp.clip(jax.random.normal(key_left, (ROWS, RANK), jnp.float32), -5.0, 5.0)
    scales = jnp.exp(jax.random.uniform(key_scale, (RANK,), jnp.float32) * math.log(1.6))
    noise = jnp.clip(jax.random.normal(key_noise, (ROWS, FFW), jnp.float32), -6.0, 6.0)
    factor = 3.0 * (math.sqrt(ROWS) + math.sqrt(FFW)) / math.sqrt(ROWS * FFW)
    signal = jnp.dot(left_factor * scales[None, :], basis.T, precision=lax.Precision.HIGHEST) * factor
    return signal + noise


def draw_sketch(key, part):
    basis = shared_basis(key)
    key = jax.random.fold_in(key, 9)
    spread = 1.5 * jnp.clip(jax.random.normal(key, (FFW, RANK), jnp.float32), -5.0, 5.0)
    return (basis + spread).astype(jnp.bfloat16)


def setup_inputs(seed: int = 0) -> dict:
    streams_of = jax.random.split(jax.random.key(seed), 3)
    return {
        "weight": draw_weight(jax.random.fold_in(streams_of[2], 71), 0),
        "sketch": draw_sketch(jax.random.fold_in(streams_of[2], 71), 0),
    }


def times_first(left, right):
    return lax.dot_general(left, right, (((0,), (0,)), ((), ())), precision=lax.Precision.HIGHEST)

def reference(weight, sketch):
    highest = lax.Precision.HIGHEST
    sketch_wide = sketch.astype(jnp.float32)
    sketch_first = jnp.dot(weight, sketch_wide, precision=highest)
    projected = times_first(weight, sketch_first)
    sketch_second = jnp.dot(weight, projected, precision=highest)
    orthonormal, upper = jnp.linalg.qr(sketch_second)
    diag_signs = jnp.sign(jnp.diagonal(upper))
    orthonormal = orthonormal * diag_signs[None, :]
    coefficient = times_first(orthonormal, weight)
    residual = (weight - jnp.dot(orthonormal, coefficient, precision=highest)).astype(jnp.bfloat16)
    left_adapter = (64.0 * orthonormal).astype(jnp.bfloat16)
    right_adapter = (coefficient / 64.0).astype(jnp.bfloat16)
    return (residual, left_adapter, right_adapter)
```

```python
import functools

import jax
import jax.numpy as jnp
from jax import lax
from jax.experimental import pallas as pl
from jax.experimental.pallas import tpu as pltpu
from jax.sharding import PartitionSpec as P

F32 = jnp.float32
BF16 = jnp.bfloat16
MIB = 1024 * 1024
VMEM = pl.BlockSpec(memory_space=pltpu.VMEM)
SMEM = pl.BlockSpec(memory_space=pltpu.SMEM)

ROWS = 2048
HALF = 1024
COLS = 896
RANK = 256
CHUNK = 128
WIDE = COLS + RANK
BLOCK = 64


def split(value):
    high = value.astype(BF16)
    return high, (value - high.astype(F32)).astype(BF16)


def dot(left, right, contract):
    return lax.dot_general(left, right, (contract, ((), ())), preferred_element_type=F32)


def dot3(left, right, contract):
    (left_high, left_low), (right_high, right_low) = left, right
    return dot(left_high, right_high, contract) + (
        dot(left_high, right_low, contract) + dot(left_low, right_high, contract)
    )


NN = ((1,), (0,))
NT = ((1,), (1,))
TN = ((0,), (0,))


def call(kernel, outs, *args, specs=None, scratch=(), limit=24):
    return pl.pallas_call(
        kernel,
        out_shape=[jax.ShapeDtypeStruct(shape, dtype) for shape, dtype in outs],
        in_specs=specs or [VMEM] * len(args),
        out_specs=[VMEM] * len(outs),
        scratch_shapes=list(scratch),
        compiler_params=pltpu.CompilerParams(vmem_limit_bytes=limit * MIB),
    )(*args)


def at(start, size, multiple):
    return pl.ds(pl.multiple_of(start, multiple), size)


def first_kernel(which_ref, weight_ref, sketch_ref, out_ref, high_ref, low_ref):
    rows = pl.ds(pl.multiple_of(pl.program_id(0) * 256, 256), 256)
    high, low = split(weight_ref[...])
    high_ref[rows, :] = high
    low_ref[rows, :] = low
    sketch = sketch_ref[...]
    out_ref[rows, :] = dot(high, sketch, NN) + dot(low, sketch, NN)


def first_product(which, weight, sketch):
    return pl.pallas_call(
        first_kernel,
        grid_spec=pltpu.PrefetchScalarGridSpec(
            num_scalar_prefetch=1,
            grid=(HALF // 256,),
            in_specs=[
                pl.BlockSpec((256, COLS), lambda i, which: (which[0] * (HALF // 256) + i, 0)),
                VMEM,
            ],
            out_specs=[VMEM] * 3,
        ),
        out_shape=[
            jax.ShapeDtypeStruct((HALF, RANK), F32),
            jax.ShapeDtypeStruct((HALF, COLS), BF16),
            jax.ShapeDtypeStruct((HALF, COLS), BF16),
        ],
        compiler_params=pltpu.CompilerParams(vmem_limit_bytes=24 * MIB),
    )(which, weight, sketch)


def permute_col(value, dy, dx, dcore):
    pairs = []
    for i in range(32):
        y, x, core = i // 8, (i // 2) % 4, i % 2
        pairs.append((i, ((y + dy) % 4) * 8 + ((x + dx) % 4) * 2 + (core ^ dcore)))
    return lax.ppermute(value, "col", pairs)


def pieces_kernel(ids_ref, keep_ref, got_ref, *outs):
    x, y = ids_ref[1], ids_ref[2]
    for r in range(4):
        rows = at(((x + r) % 4) * CHUNK, CHUNK, CHUNK)
        outs[r][...] = keep_ref[rows, :] + got_ref[rows, :]
        rows = at(4 * CHUNK + ((y + r) % 4) * CHUNK, CHUNK, CHUNK)
        outs[4 + r][...] = keep_ref[rows, :] + got_ref[rows, :]


def sum_two_kernel(a0, a1, a2, a3, b0, b1, b2, b3, a_ref, b_ref):
    a_ref[...] = (a0[...] + a2[...]) + (a1[...] + a3[...])
    b_ref[...] = (b0[...] + b2[...]) + (b1[...] + b3[...])


def sum_two_turned_kernel(a0, a1, a2, a3, b0, b1, b2, b3, a_ref, b_ref):
    a_ref[...] = ((a0[...] + a2[...]) + (a1[...] + a3[...])).T
    b_ref[...] = ((b0[...] + b2[...]) + (b1[...] + b3[...])).T


def place_kernel(ids_ref, a0, a1, a2, a3, b0, b1, b2, b3, out_ref):
    x, y = ids_ref[1], ids_ref[2]
    for r, (a, b) in enumerate(((a0, b0), (a1, b1), (a2, b2), (a3, b3))):
        out_ref[:, at(((x + 4 - r) % 4) * CHUNK, CHUNK, CHUNK)] = a[...]
        out_ref[:, at(4 * CHUNK + ((y + 4 - r) % 4) * CHUNK, CHUNK, CHUNK)] = b[...]


def sum_col(ids, keep, got):
    pieces = call(
        pieces_kernel, [((CHUNK, RANK), F32)] * 8, ids, keep, got, specs=[SMEM, VMEM, VMEM]
    )
    a = [pieces[0]] + [permute_col(pieces[r], 0, r, 0) for r in (1, 2, 3)]
    b = [pieces[4]] + [permute_col(pieces[4 + r], r, 0, 0) for r in (1, 2, 3)]
    one_a, one_b = call(sum_two_kernel, [((CHUNK, RANK), F32)] * 2, *a, *b)
    a = [one_a] + [permute_col(one_a, r, 0, 0) for r in (1, 2, 3)]
    b = [one_b] + [permute_col(one_b, 0, r, 0) for r in (1, 2, 3)]
    one_a, one_b = call(sum_two_turned_kernel, [((RANK, CHUNK), F32)] * 2, *a, *b)
    a = [one_a] + [permute_col(one_a, 0, r, 0) for r in (1, 2, 3)]
    b = [one_b] + [permute_col(one_b, r, 0, 0) for r in (1, 2, 3)]
    return call(place_kernel, [((RANK, HALF), F32)], ids, *a, *b, specs=[SMEM] + [VMEM] * 8)[0]


def permute_row(value, target):
    return lax.ppermute(value, "row", [(i, target(i) % 8) for i in range(8)])


def pair_a(z):
    return z ^ 1


def pair_b(z):
    return z + 1 if z % 2 else z - 1


def back_own_kernel(turned_ref, high_ref, low_ref, out_ref):
    out_ref[...] = dot3(split(turned_ref[...]), (high_ref[...], low_ref[...]), NN)


def back_other_kernel(
    with_gram, ids_ref, own_ref, turned_own_ref, turned_ref, high_ref, low_ref,
    a_send, b_send, a_keep, b_keep, total
):
    turned = turned_ref[...]
    total[:, :COLS] = own_ref[...] + dot3(split(turned), (high_ref[...], low_ref[...]), NN)
    if with_gram:
        total[:, COLS:] = dot3(split(turned_own_ref[...]), split(turned_own_ref[...]), NT) + dot3(
            split(turned), split(turned), NT
        )
    odd = ids_ref[3] % 2
    a_keep[...] = total[at(odd * 64, 64, 64), :]
    a_send[...] = total[at((1 - odd) * 64, 64, 64), :]
    b_keep[...] = total[at(128 + (1 - odd) * 64, 64, 64), :]
    b_send[...] = total[at(128 + odd * 64, 64, 64), :]


def quarters_kernel(ids_ref, a_keep, b_keep, a_got, b_got, *outs):
    place = ids_ref[3] // 2
    for r in range(4):
        rows = at(((place + r) % 4) * 16, 16, 16)
        outs[r][:16, :] = a_keep[rows, :] + a_got[rows, :]
        outs[r][16:, :] = b_keep[rows, :] + b_got[rows, :]


def sum_four_kernel(p0, p1, p2, p3, out_ref):
    out_ref[...] = (p0[...] + p2[...]) + (p1[...] + p3[...])


def join_kernel(ids_ref, p0, p1, p2, p3, a_ref, b_ref):
    place = ids_ref[3] // 2
    for r, p in enumerate((p0, p1, p2, p3)):
        rows = at(((place + 4 - r) % 4) * 16, 16, 16)
        a_ref[rows, :] = p[:16, :]
        b_ref[rows, :] = p[16:, :]


def back_product(ids, own, other, parts_own, parts_other, with_gram):
    width = WIDE if with_gram else COLS
    first = call(back_own_kernel, [((RANK, COLS), F32)], own, *parts_own)[0]
    band = ((64, width), F32)
    a_send, b_send, a_keep, b_keep = call(
        functools.partial(back_other_kernel, with_gram), [band] * 4,
        ids, first, own, other, *parts_other,
        specs=[SMEM] + [VMEM] * 5, scratch=[pltpu.VMEM((RANK, width), F32)],
    )
    a_got, b_got = permute_row(a_send, pair_a), permute_row(b_send, pair_b)
    part = ((32, width), F32)
    parts = call(
        quarters_kernel, [part] * 4, ids, a_keep, b_keep, a_got, b_got, specs=[SMEM] + [VMEM] * 4
    )
    parts = [parts[0]] + [permute_row(parts[r], lambda z, r=r: z + 2 * r) for r in (1, 2, 3)]
    one = call(sum_four_kernel, [part], *parts)[0]
    parts = [one] + [permute_row(one, lambda z, r=r: z + 2 * r) for r in (1, 2, 3)]
    a_band, b_band = call(join_kernel, [band] * 2, ids, *parts, specs=[SMEM] + [VMEM] * 4)
    return a_band, b_band, permute_row(a_band, pair_a), permute_row(b_band, pair_b)


def place_bands(odd, bands, columns, store):
    a_band, b_band, a_got, b_got = bands
    store(at(odd * 64, 64, 64), a_band[:, columns])
    store(at((1 - odd) * 64, 64, 64), a_got[:, columns])
    store(at(128 + (1 - odd) * 64, 64, 64), b_band[:, columns])
    store(at(128 + odd * 64, 64, 64), b_got[:, columns])


def second_send_kernel(
    ids_ref, a_band, b_band, a_got, b_got, high_ref, low_ref, out_ref, turned_high, turned_low
):
    def store(rows, value):
        turned_high[rows, :], turned_low[rows, :] = split(value)

    place_bands(ids_ref[3] % 2, (a_band, b_band, a_got, b_got), slice(None), store)
    out_ref[...] = dot3((high_ref[...], low_ref[...]), (turned_high[...], turned_low[...]), NT)


def second_keep_kernel(high_ref, low_ref, turned_high, turned_low, out_ref):
    out_ref[...] = dot3((high_ref[...], low_ref[...]), (turned_high[...], turned_low[...]), NT)


def exact_dot(left, right, contract):
    return lax.dot_general(
        left, right, (contract, ((), ())), precision=lax.Precision.HIGHEST,
        preferred_element_type=F32,
    )


def eliminate(tile, start, other):
    row_of = lax.broadcasted_iota(jnp.int32, (BLOCK, 128), 0)
    lane_of = lax.broadcasted_iota(jnp.int32, (BLOCK, 128), 1)
    for j in range(BLOCK):
        column = jnp.sum(jnp.where(lane_of == start + j, tile, 0.0), axis=1, keepdims=True)
        pivot = column[j : j + 1, :]
        row = tile[j : j + 1, :]
        scale = lax.rsqrt(pivot)
        below = jnp.where(row_of > j, column, 0.0) * (1.0 / pivot)
        tile = jnp.where(row_of == j, row * scale, tile - below * row)
    return tile


def factor_kernel(ids_ref, a_band, b_band, a_got, b_got, inverse_ref, c_ref, right_ref, work, c_work):
    def store_gram(rows, value):
        work[rows, :RANK] = value

    def store_back(rows, value):
        c_work[rows, :] = value

    bands = (a_band, b_band, a_got, b_got)
    place_bands(ids_ref[3] % 2, bands, slice(COLS, WIDE), store_gram)
    place_bands(ids_ref[3] % 2, bands, slice(0, COLS), store_back)
    rows = lax.broadcasted_iota(jnp.int32, (RANK, RANK), 0)
    lanes = lax.broadcasted_iota(jnp.int32, (RANK, RANK), 1)
    work[:, RANK:] = jnp.where(rows == lanes, 1.0, 0.0)
    row_of = lax.broadcasted_iota(jnp.int32, (BLOCK, 128), 0)
    lane_of = lax.broadcasted_iota(jnp.int32, (BLOCK, 128), 1)
    for k in range(RANK // BLOCK):
        top = k * BLOCK
        base = top // 128 * 128
        start, other = top - base, BLOCK - (top - base)
        held = (lane_of >= start) & (lane_of < start + BLOCK)
        tile = work[top : top + BLOCK, base : base + 128]
        tile = jnp.where(held, tile, jnp.where(lane_of - other == row_of, 1.0, 0.0))
        tile = eliminate(tile, start, other)
        inverse = jnp.where(held, pltpu.roll(tile, 64, 1), 0.0)
        solved = exact_dot(inverse, work[base : base + 128, :], NN)
        work[top : top + BLOCK, :] = solved
        if top + BLOCK < RANK:
            update = exact_dot(solved[:, :RANK], solved, TN)
            work[top + BLOCK :, :] = work[top + BLOCK :, :] - update[top + BLOCK :, :]
    inverse = work[:, RANK:]
    inverse_ref[...] = inverse
    coefficient = dot3(split(inverse), split(c_work[...]), NN)
    c_ref[...] = coefficient
    right_ref[...] = (coefficient * (1.0 / 64.0)).astype(BF16)


def last_kernel(ids_ref, weight_ref, own_ref, other_ref, inverse_ref, c_ref, residual_ref, left_ref, c_high, c_low):
    block = pl.program_id(0)

    @pl.when(block == 0)
    def _():
        c_high[...], c_low[...] = split(c_ref[...])

    lanes = at((block % 4) * 256, 256, 256)
    mine = (block // 4) == ids_ref[0]
    turned = jnp.where(mine, own_ref[:, lanes], other_ref[:, lanes])
    orthonormal = dot3(split(turned), split(inverse_ref[...]), ((0,), (1,)))
    left_ref[...] = (64.0 * orthonormal).astype(BF16)
    product = dot3(split(orthonormal), (c_high[...], c_low[...]), NN)
    residual_ref[...] = (weight_ref[...] - product).astype(BF16)


def last_product(ids, weight, own, other, inverse, coefficient):
    return pl.pallas_call(
        last_kernel,
        grid_spec=pltpu.PrefetchScalarGridSpec(
            num_scalar_prefetch=1,
            grid=(ROWS // 256,),
            in_specs=[pl.BlockSpec((256, COLS), lambda i, ids: (i, 0))] + [VMEM] * 4,
            out_specs=[
                pl.BlockSpec((256, COLS), lambda i, ids: (i, 0)),
                pl.BlockSpec((256, RANK), lambda i, ids: (i, 0)),
            ],
            scratch_shapes=[pltpu.VMEM((RANK, COLS), BF16)] * 2,
        ),
        out_shape=[
            jax.ShapeDtypeStruct((ROWS, COLS), BF16),
            jax.ShapeDtypeStruct((ROWS, RANK), BF16),
        ],
        compiler_params=pltpu.CompilerParams(vmem_limit_bytes=24 * MIB),
    )(ids, weight, own, other, inverse, coefficient)


def swap(value):
    return permute_col(value, 0, 0, 1)


def per_device(weight, sketch):
    col, z = lax.axis_index("col"), lax.axis_index("row")
    core, x, y = col % 2, (col // 2) % 4, col // 8
    ids = jnp.stack([core, x, y, z]).astype(jnp.int32)
    away = jnp.stack([1 - core]).astype(jnp.int32)

    send, *parts_other = first_product(away, weight, sketch)
    got = swap(send)
    keep, *parts_own = first_product(ids, weight, sketch)
    own = sum_col(ids, keep, got)
    other = swap(own)
    bands = back_product(ids, own, other, parts_own, parts_other, False)

    turned = ((RANK, COLS), BF16)
    send, *projected = call(
        second_send_kernel, [((HALF, RANK), F32), turned, turned], ids, *bands, *parts_other,
        specs=[SMEM] + [VMEM] * 6,
    )
    got = swap(send)
    keep = call(second_keep_kernel, [((HALF, RANK), F32)], *parts_own, *projected)[0]
    own = sum_col(ids, keep, got)
    other = swap(own)
    bands = back_product(ids, own, other, parts_own, parts_other, True)

    inverse, coefficient, right_adapter = call(
        factor_kernel,
        [((RANK, RANK), F32), ((RANK, COLS), F32), ((RANK, COLS), BF16)],
        ids, *bands, specs=[SMEM] + [VMEM] * 4,
        scratch=[pltpu.VMEM((RANK, 2 * RANK), F32), pltpu.VMEM((RANK, COLS), F32)],
    )
    residual, left_adapter = last_product(ids, weight, own, other, inverse, coefficient)
    return (residual, left_adapter, right_adapter)


def solution(mesh):
    return jax.shard_map(
        per_device,
        mesh=mesh,
        in_specs=(P("row", "col"), P("col", None)),
        out_specs=(P("row", "col"), P("row", None), P(None, "col")),
        check_vma=False,
    )
```

```python
import functools

import jax
import jax.numpy as jnp
from jax import lax
from jax.experimental import pallas as pl
from jax.experimental.pallas import tpu as pltpu
from jax.sharding import PartitionSpec as P

F32 = jnp.float32
BF16 = jnp.bfloat16
MIB = 1024 * 1024
VMEM = pl.BlockSpec(memory_space=pltpu.VMEM)
ANY = pl.BlockSpec(memory_space=pl.ANY)

ROWS = 2048
HALF = 1024
COLS = 896
RANK = 256
CHUNK = 256
BAND = 128
QUARTER = 32
BLOCK = 64
GROUP = 4


def split(value):
    high = value.astype(BF16)
    return high, (value - high.astype(F32)).astype(BF16)


def dot(left, right, contract):
    return lax.dot_general(left, right, (contract, ((), ())), preferred_element_type=F32)


def dot3(left, right, contract):
    (left_high, left_low), (right_high, right_low) = left, right
    return dot(left_high, right_high, contract) + (
        dot(left_high, right_low, contract) + dot(left_low, right_high, contract)
    )


NN = ((1,), (0,))
NT = ((1,), (1,))
TN = ((0,), (0,))


def call(kernel, outs, *args, specs=None, scratch=(), limit=24):
    return pl.pallas_call(
        kernel,
        out_shape=[jax.ShapeDtypeStruct(shape, dtype) for shape, dtype in outs],
        in_specs=specs or [VMEM] * len(args),
        out_specs=[VMEM] * len(outs),
        scratch_shapes=list(scratch),
        compiler_params=pltpu.CompilerParams(vmem_limit_bytes=limit * MIB),
    )(*args)


def here():
    col = lax.axis_index("col")
    return col & 1, (col >> 1) & 3, col >> 3, lax.axis_index("row")


def first_axis():
    core, x, y, _ = here()
    return jnp.where(core == 0, x, y)


def kept_half(level):
    core, _, _, z = here()
    if level == 0:
        return (z + core) & 1
    place = ((z >> 1) + core) & 3
    return ((place + 1) >> 1) & 1 if level == 1 else place >> 1


def at(start, size, multiple):
    return pl.ds(pl.multiple_of(start, multiple), size)


PIECE = 256


def fetch(half, weight_ref, to_ref, sems):
    copies = []
    for i in range(HALF // PIECE):
        rows = at(half * HALF + i * PIECE, PIECE, PIECE)
        here_rows = pl.ds(i * PIECE, PIECE)
        copies.append(
            pltpu.make_async_copy(weight_ref.at[rows, :], to_ref.at[here_rows, :], sems.at[i])
        )
    for copy in copies:
        copy.start()
    return copies


def first_kernel(away, weight_ref, sketch_hbm, out_ref, high_ref, low_ref, held, sketch_ref, sems):
    core = here()[0]
    sketch_copy = pltpu.make_async_copy(sketch_hbm, sketch_ref, sems.at[HALF // PIECE])
    sketch_copy.start()
    copies = fetch(1 - core if away else core, weight_ref, held, sems)
    sketch_copy.wait()
    for i in range(HALF // PIECE):
        copies[i].wait()
        first_piece(i, held, sketch_ref, out_ref, high_ref, low_ref)


def first_piece(i, weight_ref, sketch_ref, out_ref, high_ref, low_ref):
    rows = slice(i * PIECE, (i + 1) * PIECE)
    high, low = split(weight_ref[rows, :])
    high_ref[rows, :] = high
    low_ref[rows, :] = low
    sketch = sketch_ref[...]
    out_ref[rows, :] = dot(high, sketch, NN) + dot(low, sketch, NN)


def first_product(away, weight, sketch):
    return call(
        functools.partial(first_kernel, away),
        [((HALF, RANK), F32), ((HALF, COLS), BF16), ((HALF, COLS), BF16)], weight, sketch,
        specs=[ANY, ANY],
        scratch=[
            pltpu.VMEM((HALF, COLS), F32), pltpu.VMEM((COLS, RANK), BF16),
            pltpu.SemaphoreType.DMA((HALF // PIECE + 1,)),
        ],
        limit=48,
    )


def swap(value):
    return lax.ppermute(value, "col", [(i, i ^ 1) for i in range(32)])


def permute_plane(value, step, first):
    pairs = []
    for i in range(32):
        y, x, core = i // 8, (i // 2) % 4, i % 2
        if (core == 0) == first:
            x = (x + step) % 4
        else:
            y = (y + step) % 4
        pairs.append((i, y * 8 + x * 2 + core))
    return lax.ppermute(value, "col", pairs)


def exchange(pieces, first):
    return [pieces[0]] + [permute_plane(pieces[r], r, first) for r in (1, 2, 3)]


def pieces_kernel(keep_ref, got_ref, *outs):
    for r in range(4):
        rows = at(((first_axis() + r) & 3) * CHUNK, CHUNK, CHUNK)
        outs[r][...] = keep_ref[rows, :] + got_ref[rows, :]


def sum_four(p0, p1, p2, p3):
    return (p0[...] + p2[...]) + (p1[...] + p3[...])


def sum_kernel(p0, p1, p2, p3, out_ref):
    out_ref[...] = sum_four(p0, p1, p2, p3)


def sum_turned_kernel(p0, p1, p2, p3, out_ref):
    out_ref[...] = sum_four(p0, p1, p2, p3).T


def place_kernel(p0, p1, p2, p3, out_ref):
    for r, p in enumerate((p0, p1, p2, p3)):
        out_ref[:, at(((first_axis() + 4 - r) & 3) * CHUNK, CHUNK, CHUNK)] = p[...]


def sum_col(keep, got):
    piece = ((CHUNK, RANK), F32)
    pieces = call(pieces_kernel, [piece] * 4, keep, got)
    one = call(sum_kernel, [piece], *exchange(pieces, True))[0]
    one = call(sum_turned_kernel, [piece], *exchange([one] * 4, False))[0]
    pieces = exchange([one] * 4, True)
    return call(place_kernel, [((RANK, HALF), F32)], *pieces)[0]


def permute_halving(value, level):
    pairs = []
    for z in range(8):
        for i in range(32):
            core, place = i % 2, (z // 2 + i % 2) % 4
            if level == 0:
                other = z + 1 if z % 2 == core else z - 1
            else:
                partner = place ^ 1 if level == 1 else 3 - place
                other = (partner - core) % 4 * 2 + z % 2
            pairs.append((z * 32 + i, other % 8 * 32 + i))
    return lax.ppermute(value, ("row", "col"), pairs)


def halve(total, kept, size, send_ref, keep_ref):
    keep_ref[...] = total[at(kept * size, size, size), :]
    send_ref[...] = total[at((1 - kept) * size, size, size), :]


def back_own_kernel(turned_ref, high_ref, low_ref, out_ref):
    out_ref[...] = dot3(split(turned_ref[...]), (high_ref[...], low_ref[...]), NN)


def back_other_kernel(own_ref, turned_ref, high_ref, low_ref, _, send_ref, keep_ref, total):
    total[...] = own_ref[...] + dot3(split(turned_ref[...]), (high_ref[...], low_ref[...]), NN)
    halve(total, kept_half(0), BAND, send_ref, keep_ref)


def halve_kernel(level, keep_ref, got_ref, _, send_out, keep_out, total):
    total[...] = keep_ref[...] + got_ref[...]
    halve(total, kept_half(level), BAND >> level, send_out, keep_out)


def add_kernel(left_ref, right_ref, out_ref):
    out_ref[...] = left_ref[...] + right_ref[...]


def add_after_kernel(left_ref, right_ref, _, out_ref):
    out_ref[...] = left_ref[...] + right_ref[...]


def join_kernel(level, keep_ref, got_ref, _, out_ref):
    kept, size = kept_half(level), BAND >> level
    out_ref[at(kept * size, size, size), :] = keep_ref[...]
    out_ref[at((1 - kept) * size, size, size), :] = got_ref[...]


def back_product(first, other, parts_other, side):
    mark = next(side)

    def rows(size):
        return ((size, COLS), F32)

    send, keep = call(
        back_other_kernel, [rows(BAND)] * 2, first, other, *parts_other, mark,
        specs=[VMEM] * 4 + [ANY], scratch=[pltpu.VMEM((RANK, COLS), F32)],
    )
    specs = [VMEM] * 2 + [ANY]
    for level in (1, 2):
        got = permute_halving(send, level - 1)
        send, keep = call(
            functools.partial(halve_kernel, level), [rows(BAND >> level)] * 2,
            keep, got, next(side),
            specs=specs, scratch=[pltpu.VMEM((2 * BAND >> level, COLS), F32)],
        )
    got = permute_halving(send, 2)
    keep = call(add_after_kernel, [rows(QUARTER)], keep, got, next(side), specs=specs)[0]
    for level in (2, 1):
        got = permute_halving(keep, level)
        keep = call(
            functools.partial(join_kernel, level), [rows(2 * BAND >> level)],
            keep, got, next(side), specs=specs,
        )[0]
    return keep, permute_halving(keep, 0)


def second_send_kernel(band, got, high_ref, low_ref, out_ref, turned_high, turned_low):
    kept = kept_half(0)
    for half, value in ((kept, band), (1 - kept, got)):
        rows = at(half * BAND, BAND, BAND)
        turned_high[rows, :], turned_low[rows, :] = split(value[...])
    out_ref[...] = dot3((high_ref[...], low_ref[...]), (turned_high[...], turned_low[...]), NT)


def second_keep_kernel(high_ref, low_ref, turned_high, turned_low, out_ref):
    out_ref[...] = dot3((high_ref[...], low_ref[...]), (turned_high[...], turned_low[...]), NT)


def gram_kernel(own_ref, other_ref, out_ref):
    rows = at(here()[0] * BAND + here()[1] * QUARTER, QUARTER, QUARTER)
    out_ref[...] = dot3(split(own_ref[rows, :]), split(own_ref[...]), NT) + dot3(
        split(other_ref[rows, :]), split(other_ref[...]), NT
    )


def place_gram_kernel(p0, p1, p2, p3, out_ref):
    for r, p in enumerate((p0, p1, p2, p3)):
        out_ref[at(((here()[1] + 4 - r) & 3) * QUARTER, QUARTER, QUARTER), :] = p[...]


def permute_x(value, step):
    return lax.ppermute(
        value, "col", [(i, i // 8 * 8 + (i % 8 + 2 * step) % 8) for i in range(32)]
    )


def exchange_parity(value):
    return [value] + [
        lax.ppermute(value, "row", [(z, (z + 2 * r) % 8) for z in range(8)]) for r in (1, 2, 3)
    ]


def gram_and_factor(own, other, results):
    piece = ((QUARTER, RANK), F32)
    one = call(gram_kernel, [piece], own, other)[0]
    yield one
    one = call(add_kernel, [piece], one, permute_halving(one, 0))[0]
    yield one
    one = call(sum_kernel, [piece], *exchange_parity(one))[0]
    yield one
    pieces = [one] + [permute_x(one, r) for r in (1, 2, 3)]
    half = call(
        place_gram_kernel, [((BAND, RANK), F32)], *pieces
    )[0]
    yield half
    wide = ((RANK, 2 * RANK), F32)
    half_done = call(
        factor_first_kernel, [wide], half, swap(half)
    )[0]
    yield half_done
    inverse = call(
        factor_last_kernel, [((RANK, RANK), BF16)] * 2, half_done,
        scratch=[pltpu.VMEM((RANK, 2 * RANK), F32)],
    )
    yield inverse[0]
    basis = ((ROWS, RANK), BF16)
    results += inverse + call(
        basis_kernel, [basis] * 3, own, other, *inverse
    )


def exact_dot(left, right, contract):
    return lax.dot_general(
        left, right, (contract, ((), ())), precision=lax.Precision.HIGHEST,
        preferred_element_type=F32,
    )


def eliminate(tile, start):
    row_of = lax.broadcasted_iota(jnp.int32, (BLOCK, 128), 0)
    for j in range(0, BLOCK, GROUP):
        columns = [
            jnp.broadcast_to(tile[:, start + j + m : start + j + m + 1], (BLOCK, 128))
            for m in range(GROUP)
        ]
        rows = [tile[j + m : j + m + 1, :] for m in range(GROUP)]
        scales = []
        for m in range(GROUP):
            pivot = columns[m][j + m : j + m + 1, :]
            inverse = 1.0 / pivot
            scales.append(lax.rsqrt(pivot))
            for n in range(m + 1, GROUP):
                rows[n] = rows[n] - rows[m] * (columns[m][j + n : j + n + 1, :] * inverse)
                columns[n] = columns[n] - columns[m] * (columns[n][j + m : j + m + 1, :] * inverse)
            columns[m] = jnp.where(row_of > j + m, columns[m], 0.0) * inverse
        for m in range(GROUP):
            tile = tile - columns[m] * rows[m]
        for m in range(GROUP):
            tile = jnp.where(row_of == j + m, rows[m] * scales[m], tile)
    return tile


def factor_block(work, k):
    row_of = lax.broadcasted_iota(jnp.int32, (BLOCK, 128), 0)
    lane_of = lax.broadcasted_iota(jnp.int32, (BLOCK, 128), 1)
    top = k * BLOCK
    base = top // 128 * 128
    start, other = top - base, BLOCK - (top - base)
    held = (lane_of >= start) & (lane_of < start + BLOCK)
    tile = work[top : top + BLOCK, base : base + 128]
    tile = jnp.where(held, tile, jnp.where(lane_of - other == row_of, 1.0, 0.0))
    tile = eliminate(tile, start)
    inverse = jnp.where(held, pltpu.roll(tile, 64, 1), 0.0)
    solved = exact_dot(inverse, work[base : base + 128, :], NN)
    work[top : top + BLOCK, :] = solved
    if top + BLOCK < RANK:
        update = exact_dot(solved[:, :RANK], solved, TN)
        work[top + BLOCK :, :] = work[top + BLOCK :, :] - update[top + BLOCK :, :]


def factor_first_kernel(half_ref, got_ref, work):
    core = here()[0]
    work[at(core * BAND, BAND, BAND), :RANK] = half_ref[...]
    work[at((1 - core) * BAND, BAND, BAND), :RANK] = got_ref[...]
    rows = lax.broadcasted_iota(jnp.int32, (RANK, RANK), 0)
    lanes = lax.broadcasted_iota(jnp.int32, (RANK, RANK), 1)
    work[:, RANK:] = jnp.where(rows == lanes, 1.0, 0.0)
    factor_block(work, 0)
    factor_block(work, 1)


def factor_last_kernel(half_done, inverse_high, inverse_low, work):
    work[...] = half_done[...]
    factor_block(work, 2)
    factor_block(work, 3)
    inverse_high[...], inverse_low[...] = split(work[:, RANK:])


def basis_kernel(own_ref, other_ref, inverse_high, inverse_low, left_ref, high_ref, low_ref):
    inverse = inverse_high[...], inverse_low[...]
    for half, ref in ((here()[0], own_ref), (1 - here()[0], other_ref)):
        for k in range(HALF // 256):
            rows = at(half * HALF + k * 256, 256, 256)
            orthonormal = dot3(split(ref[:, k * 256 : (k + 1) * 256].T), inverse, NT)
            left_ref[rows, :] = (64.0 * orthonormal).astype(BF16)
            high_ref[rows, :], low_ref[rows, :] = split(orthonormal)


STEP = 512


def last_kernel(
    weight_ref, basis_high, basis_low, inverse_high, inverse_low, band, got,
    residual_ref, right_ref, z_work, c_high, c_low
):
    @pl.when(pl.program_id(0) == 0)
    def _():
        kept = kept_half(0)
        z_work[at(kept * BAND, BAND, BAND), :] = band[...]
        z_work[at((1 - kept) * BAND, BAND, BAND), :] = got[...]
        coefficient = dot3((inverse_high[...], inverse_low[...]), split(z_work[...]), NN)
        right_ref[...] = (coefficient * (1.0 / 64.0)).astype(BF16)
        c_high[...], c_low[...] = split(coefficient)

    product = dot3((basis_high[...], basis_low[...]), (c_high[...], c_low[...]), NN)
    residual_ref[...] = (weight_ref[...] - product).astype(BF16)


def last_product(weight, basis, inverse, band, got):
    def rows(width):
        return pl.BlockSpec((STEP, width), lambda i: (i, 0))

    return pl.pallas_call(
        last_kernel,
        grid=(ROWS // STEP,),
        in_specs=[rows(COLS), rows(RANK), rows(RANK)] + [VMEM] * 4,
        out_specs=[rows(COLS), VMEM],
        scratch_shapes=[pltpu.VMEM((RANK, COLS), F32)] + [pltpu.VMEM((RANK, COLS), BF16)] * 2,
        out_shape=[
            jax.ShapeDtypeStruct((ROWS, COLS), BF16),
            jax.ShapeDtypeStruct((RANK, COLS), BF16),
        ],
        compiler_params=pltpu.CompilerParams(vmem_limit_bytes=24 * MIB),
    )(weight, *basis, *inverse, band, got)


def per_device(weight, sketch):
    send, *parts_other = first_product(True, weight, sketch)
    got = swap(send)
    keep, *parts_own = first_product(False, weight, sketch)
    own = sum_col(keep, got)
    other = swap(own)
    first = call(back_own_kernel, [((RANK, COLS), F32)], own, *parts_own)[0]
    bands = back_product(first, other, parts_other, iter([first] * 6))

    turned = ((RANK, COLS), BF16)
    send, *projected = call(
        second_send_kernel, [((HALF, RANK), F32), turned, turned], *bands, *parts_other
    )
    got = swap(send)
    keep = call(second_keep_kernel, [((HALF, RANK), F32)], *parts_own, *projected)[0]
    own = sum_col(keep, got)
    other = swap(own)
    first = call(back_own_kernel, [((RANK, COLS), F32)], own, *parts_own)[0]
    results = []
    side = gram_and_factor(own, other, results)
    bands = back_product(first, other, parts_other, side)
    next(side, None)
    inverse, left_adapter, basis = results[:2], results[2], results[3:]
    residual, right_adapter = last_product(weight, basis, inverse, *bands)
    return residual, left_adapter, right_adapter


def solution(mesh):
    return jax.shard_map(
        per_device,
        mesh=mesh,
        in_specs=(P("row", "col"), P("col", None)),
        out_specs=(P("row", "col"), P("row", None), P(None, "col")),
        check_vma=False,
    )
```

```python
import functools

import jax
import jax.numpy as jnp
from jax import lax
from jax.experimental import pallas as pl
from jax.experimental.pallas import tpu as pltpu
from jax.sharding import PartitionSpec as P

F32 = jnp.float32
BF16 = jnp.bfloat16
MIB = 1024 * 1024
VMEM = pl.BlockSpec(memory_space=pltpu.VMEM)
ANY = pl.BlockSpec(memory_space=pl.ANY)
HBM = pl.BlockSpec(memory_space=pltpu.HBM)

ROWS = 2048
HALF = 1024
COLS = 896
RANK = 256
CHUNK = 256
BAND = 128
PART = 64
QUARTER = 32
BLOCK = 64
GROUP = 4


def split(value):
    high = value.astype(BF16)
    return high, (value - high.astype(F32)).astype(BF16)


def dot(left, right, contract):
    return lax.dot_general(left, right, (contract, ((), ())), preferred_element_type=F32)


def dot3(left, right, contract):
    (left_high, left_low), (right_high, right_low) = left, right
    return dot(left_high, right_high, contract) + (
        dot(left_high, right_low, contract) + dot(left_low, right_high, contract)
    )


NN = ((1,), (0,))
NT = ((1,), (1,))
TN = ((0,), (0,))


def call(kernel, outs, *args, specs=None, out_specs=None, scratch=(), limit=24):
    return pl.pallas_call(
        kernel,
        out_shape=[jax.ShapeDtypeStruct(shape, dtype) for shape, dtype in outs],
        in_specs=specs or [VMEM] * len(args),
        out_specs=out_specs or [VMEM] * len(outs),
        scratch_shapes=list(scratch),
        compiler_params=pltpu.CompilerParams(vmem_limit_bytes=limit * MIB),
    )(*args)


def here():
    col = lax.axis_index("col")
    return col & 1, (col >> 1) & 3, col >> 3, lax.axis_index("row")


def first_axis():
    core, x, y, _ = here()
    return jnp.where(core == 0, x, y)


def kept_half(level):
    core, _, _, z = here()
    if level == 0:
        return (z + core) & 1
    place = ((z >> 1) + core) & 3
    return ((place + 1) >> 1) & 1


def at(start, size, multiple):
    return pl.ds(pl.multiple_of(start, multiple), size)


PIECE = 256


def first_kernel(away, weight_ref, sketch_ref, out_ref, high_ref, low_ref):
    core = here()[0]
    half = 1 - core if away else core
    for i in range(HALF // PIECE):
        rows = slice(i * PIECE, (i + 1) * PIECE)
        high, low = split(weight_ref[at(half * HALF + i * PIECE, PIECE, PIECE), :])
        high_ref[rows, :] = high
        low_ref[rows, :] = low
        sketch = sketch_ref[...]
        out_ref[rows, :] = dot(high, sketch, NN) + dot(low, sketch, NN)


def first_product(away, weight, sketch):
    return call(
        functools.partial(first_kernel, away),
        [((HALF, RANK), F32), ((HALF, COLS), BF16), ((HALF, COLS), BF16)], weight, sketch,
    )


def swap(value):
    return lax.ppermute(value, "col", [(i, i ^ 1) for i in range(32)])


def permute_plane(value, step, first):
    pairs = []
    for i in range(32):
        y, x, core = i // 8, (i // 2) % 4, i % 2
        if (core == 0) == first:
            x = (x + step) % 4
        else:
            y = (y + step) % 4
        pairs.append((i, y * 8 + x * 2 + core))
    return lax.ppermute(value, "col", pairs)


def exchange(pieces, first):
    return [pieces[0]] + [permute_plane(pieces[r], r, first) for r in (1, 2, 3)]


def pieces_kernel(keep_ref, got_ref, *outs):
    for r in range(4):
        rows = at(((first_axis() + r) & 3) * CHUNK, CHUNK, CHUNK)
        outs[r][...] = keep_ref[rows, :] + got_ref[rows, :]


def sum_four(p0, p1, p2, p3):
    return (p0[...] + p2[...]) + (p1[...] + p3[...])


def sum_kernel(p0, p1, p2, p3, *outs):
    for out_ref in outs:
        out_ref[...] = sum_four(p0, p1, p2, p3)


def sum_turned_kernel(p0, p1, p2, p3, *outs):
    total = sum_four(p0, p1, p2, p3).T
    for out_ref in outs:
        out_ref[...] = total


def place_kernel(p0, p1, p2, p3, out_ref):
    for r, p in enumerate((p0, p1, p2, p3)):
        out_ref[:, at(((first_axis() + 4 - r) & 3) * CHUNK, CHUNK, CHUNK)] = p[...]


def sum_col(keep, got):
    piece = ((CHUNK, RANK), F32)
    pieces = call(pieces_kernel, [piece] * 4, keep, got)
    ones = call(sum_kernel, [piece] * 3, *exchange(pieces, True))
    ones = call(sum_turned_kernel, [piece] * 3, *exchange(ones[:1] + ones, False))
    pieces = exchange(ones[:1] + ones, True)
    return call(place_kernel, [((RANK, HALF), F32)], *pieces)[0]


def permute_halving(value, level):
    pairs = []
    for z in range(8):
        for i in range(32):
            core, place = i % 2, (z // 2 + i % 2) % 4
            if level == 0:
                other = z + 1 if z % 2 == core else z - 1
            else:
                partner = place ^ 1 if level == 1 else 3 - place
                other = (partner - core) % 4 * 2 + z % 2
            pairs.append((z * 32 + i, other % 8 * 32 + i))
    return lax.ppermute(value, ("row", "col"), pairs)


def halve(total, kept, size, send_ref, keep_ref):
    keep_ref[...] = total[at(kept * size, size, size), :]
    send_ref[...] = total[at((1 - kept) * size, size, size), :]


def back_own_kernel(turned_ref, high_ref, low_ref, out_ref):
    out_ref[...] = dot3(split(turned_ref[...]), (high_ref[...], low_ref[...]), NN)


def back_other_kernel(own_ref, turned_ref, high_ref, low_ref, out_ref):
    out_ref[...] = own_ref[...] + dot3(split(turned_ref[...]), (high_ref[...], low_ref[...]), NN)


def halve_first_kernel(total, _, send_ref, keep_ref):
    halve(total, kept_half(0), BAND, send_ref, keep_ref)


def halve_kernel(keep_ref, got_ref, _, send_out, keep_out, total):
    total[...] = keep_ref[...] + got_ref[...]
    halve(total, kept_half(1), PART, send_out, keep_out)


def add_kernel(left_ref, right_ref, *outs):
    for out_ref in outs:
        out_ref[...] = left_ref[...] + right_ref[...]


def add_after_kernel(left_ref, right_ref, _, out_ref):
    out_ref[...] = left_ref[...] + right_ref[...]


def join_kernel(keep_ref, got_ref, _, out_ref):
    kept = kept_half(1)
    out_ref[at(kept * PART, PART, PART), :] = keep_ref[...]
    out_ref[at((1 - kept) * PART, PART, PART), :] = got_ref[...]


def back_product(first, other, parts_other, side):
    whole, band, part = ((RANK, COLS), F32), ((BAND, COLS), F32), ((PART, COLS), F32)
    specs = [VMEM] * 2 + [ANY]
    total = call(back_other_kernel, [whole], first, other, *parts_other)[0]
    send, keep = call(halve_first_kernel, [band] * 2, total, next(side), specs=specs[1:])
    got = permute_halving(send, 0)
    send, keep = call(
        halve_kernel, [part] * 2, keep, got, next(side),
        specs=specs, scratch=[pltpu.VMEM((BAND, COLS), F32)],
    )
    got = permute_halving(send, 1)
    keep = call(add_after_kernel, [part], keep, got, next(side), specs=specs)[0]
    got = permute_halving(keep, 2)
    keep = call(add_after_kernel, [part], keep, got, next(side), specs=specs)[0]
    got = permute_halving(keep, 1)
    keep = call(join_kernel, [band], keep, got, next(side), specs=specs)[0]
    return keep, permute_halving(keep, 0)


def second_send_kernel(band, got, high_ref, low_ref, out_ref, turned_high, turned_low):
    kept = kept_half(0)
    for half, value in ((kept, band), (1 - kept, got)):
        rows = at(half * BAND, BAND, BAND)
        turned_high[rows, :], turned_low[rows, :] = split(value[...])
    out_ref[...] = dot3((high_ref[...], low_ref[...]), (turned_high[...], turned_low[...]), NT)


def second_keep_kernel(high_ref, low_ref, turned_high, turned_low, out_ref):
    out_ref[...] = dot3((high_ref[...], low_ref[...]), (turned_high[...], turned_low[...]), NT)


def gram_kernel(own_ref, other_ref, out_ref):
    rows = at(here()[0] * BAND + here()[1] * QUARTER, QUARTER, QUARTER)
    out_ref[...] = dot3(split(own_ref[rows, :]), split(own_ref[...]), NT) + dot3(
        split(other_ref[rows, :]), split(other_ref[...]), NT
    )


def place_gram_kernel(p0, p1, p2, p3, out_ref):
    for r, p in enumerate((p0, p1, p2, p3)):
        out_ref[at(((here()[1] + 4 - r) & 3) * QUARTER, QUARTER, QUARTER), :] = p[...]


def permute_x(value, step):
    return lax.ppermute(
        value, "col", [(i, i // 8 * 8 + (i % 8 + 2 * step) % 8) for i in range(32)]
    )


def gram_and_factor(own, other, results):
    piece = ((QUARTER, RANK), F32)
    one = call(gram_kernel, [piece], own, other)[0]
    for level in range(3):
        got = permute_halving(one, level)
        ones = call(add_kernel, [piece] * (3 if level == 2 else 1), one, got)
        one = ones[0]
        yield one
    pieces = [one] + [permute_x(ones[r - 1], r) for r in (1, 2, 3)]
    half = call(
        place_gram_kernel, [((BAND, RANK), F32)], *pieces
    )[0]
    yield half
    wide = ((RANK, 2 * RANK), F32)
    half_done = call(
        factor_first_kernel, [wide], half, swap(half)
    )[0]
    yield half_done
    inverse = call(
        factor_last_kernel, [((RANK, RANK), BF16)] * 2, half_done,
        scratch=[pltpu.VMEM((RANK, 2 * RANK), F32)],
    )
    basis = ((ROWS, RANK), BF16)
    results += inverse + call(
        basis_kernel, [basis] * 3, own, other, *inverse
    )


def exact_dot(left, right, contract):
    return lax.dot_general(
        left, right, (contract, ((), ())), precision=lax.Precision.HIGHEST,
        preferred_element_type=F32,
    )


def eliminate(tile, start):
    row_of = lax.broadcasted_iota(jnp.int32, (BLOCK, 128), 0)
    for j in range(0, BLOCK, GROUP):
        columns = [
            jnp.broadcast_to(tile[:, start + j + m : start + j + m + 1], (BLOCK, 128))
            for m in range(GROUP)
        ]
        rows = [tile[j + m : j + m + 1, :] for m in range(GROUP)]
        scales = []
        for m in range(GROUP):
            pivot = columns[m][j + m : j + m + 1, :]
            inverse = 1.0 / pivot
            scales.append(lax.rsqrt(pivot))
            for n in range(m + 1, GROUP):
                rows[n] = rows[n] - rows[m] * (columns[m][j + n : j + n + 1, :] * inverse)
                columns[n] = columns[n] - columns[m] * (columns[n][j + m : j + m + 1, :] * inverse)
            columns[m] = jnp.where(row_of > j + m, columns[m], 0.0) * inverse
        for m in range(GROUP):
            tile = tile - columns[m] * rows[m]
        for m in range(GROUP):
            tile = jnp.where(row_of == j + m, rows[m] * scales[m], tile)
    return tile


def factor_block(work, k):
    row_of = lax.broadcasted_iota(jnp.int32, (BLOCK, 128), 0)
    lane_of = lax.broadcasted_iota(jnp.int32, (BLOCK, 128), 1)
    top = k * BLOCK
    base = top // 128 * 128
    start, other = top - base, BLOCK - (top - base)
    held = (lane_of >= start) & (lane_of < start + BLOCK)
    tile = work[top : top + BLOCK, base : base + 128]
    tile = jnp.where(held, tile, jnp.where(lane_of - other == row_of, 1.0, 0.0))
    tile = eliminate(tile, start)
    inverse = jnp.where(held, pltpu.roll(tile, 64, 1), 0.0)
    solved = exact_dot(inverse, work[base : base + 128, :], NN)
    work[top : top + BLOCK, :] = solved
    if top + BLOCK < RANK:
        update = exact_dot(solved[:, :RANK], solved, TN)
        work[top + BLOCK :, :] = work[top + BLOCK :, :] - update[top + BLOCK :, :]


def factor_first_kernel(half_ref, got_ref, work):
    core = here()[0]
    work[at(core * BAND, BAND, BAND), :RANK] = half_ref[...]
    work[at((1 - core) * BAND, BAND, BAND), :RANK] = got_ref[...]
    rows = lax.broadcasted_iota(jnp.int32, (RANK, RANK), 0)
    lanes = lax.broadcasted_iota(jnp.int32, (RANK, RANK), 1)
    work[:, RANK:] = jnp.where(rows == lanes, 1.0, 0.0)
    factor_block(work, 0)
    factor_block(work, 1)


def factor_last_kernel(half_done, inverse_high, inverse_low, work):
    work[...] = half_done[...]
    factor_block(work, 2)
    factor_block(work, 3)
    inverse_high[...], inverse_low[...] = split(work[:, RANK:])


def basis_kernel(own_ref, other_ref, inverse_high, inverse_low, left_ref, high_ref, low_ref):
    inverse = inverse_high[...], inverse_low[...]
    for half, ref in ((here()[0], own_ref), (1 - here()[0], other_ref)):
        for k in range(HALF // 256):
            rows = at(half * HALF + k * 256, 256, 256)
            orthonormal = dot3(split(ref[:, k * 256 : (k + 1) * 256].T), inverse, NT)
            left_ref[rows, :] = (64.0 * orthonormal).astype(BF16)
            high_ref[rows, :], low_ref[rows, :] = split(orthonormal)


STEP = 512


def last_kernel(
    own_high, own_low, other_high, other_low, basis_high, basis_low, inverse_high, inverse_low,
    band, got, residual_ref, right_ref, z_work, c_high, c_low, held, sems
):
    core, kept = here()[0], kept_half(0)
    z_work[at(kept * BAND, BAND, BAND), :] = band[...]
    z_work[at((1 - kept) * BAND, BAND, BAND), :] = got[...]
    coefficient = dot3((inverse_high[...], inverse_low[...]), split(z_work[...]), NN)
    right_ref[...] = (coefficient * (1.0 / 64.0)).astype(BF16)
    c_high[...], c_low[...] = split(coefficient)
    copies = []
    for half, high, low in ((core, own_high, own_low), (1 - core, other_high, other_low)):
        for k in range(HALF // STEP):
            rows = at(half * HALF + k * STEP, STEP, STEP)
            here_rows = slice(k * STEP, (k + 1) * STEP)
            slot = held.at[len(copies)]
            product = dot3((basis_high[rows, :], basis_low[rows, :]), (c_high[...], c_low[...]), NN)
            weight = high[here_rows, :].astype(F32) + low[here_rows, :].astype(F32)
            slot[...] = (weight - product).astype(BF16)
            copies.append(
                pltpu.make_async_copy(slot, residual_ref.at[rows, :], sems.at[len(copies)])
            )
            copies[-1].start()
    for copy in copies:
        copy.wait()


def last_product(parts_own, parts_other, basis, inverse, band, got):
    steps = ROWS // STEP
    return call(
        last_kernel, [((ROWS, COLS), BF16), ((RANK, COLS), BF16)],
        *parts_own, *parts_other, *basis, *inverse, band, got,
        out_specs=[HBM, VMEM],
        scratch=[
            pltpu.VMEM((RANK, COLS), F32), pltpu.VMEM((RANK, COLS), BF16),
            pltpu.VMEM((RANK, COLS), BF16), pltpu.VMEM((steps, STEP, COLS), BF16),
            pltpu.SemaphoreType.DMA((steps,)),
        ],
    )


def per_device(weight, sketch):
    send, *parts_other = first_product(True, weight, sketch)
    got = swap(send)
    keep, *parts_own = first_product(False, weight, sketch)
    own = sum_col(keep, got)
    other = swap(own)
    first = call(back_own_kernel, [((RANK, COLS), F32)], own, *parts_own)[0]
    bands = back_product(first, other, parts_other, iter([first] * 5))

    turned = ((RANK, COLS), BF16)
    send, *projected = call(
        second_send_kernel, [((HALF, RANK), F32), turned, turned], *bands, *parts_other
    )
    got = swap(send)
    keep = call(second_keep_kernel, [((HALF, RANK), F32)], *parts_own, *projected)[0]
    own = sum_col(keep, got)
    other = swap(own)
    first = call(back_own_kernel, [((RANK, COLS), F32)], own, *parts_own)[0]
    results = []
    side = gram_and_factor(own, other, results)
    bands = back_product(first, other, parts_other, side)
    next(side, None)
    inverse, left_adapter, basis = results[:2], results[2], results[3:]
    residual, right_adapter = last_product(
        parts_own, parts_other, basis, inverse, *bands
    )
    return residual, left_adapter, right_adapter


def solution(mesh):
    return jax.shard_map(
        per_device,
        mesh=mesh,
        in_specs=(P("row", "col"), P("col", None)),
        out_specs=(P("row", "col"), P("row", None), P(None, "col")),
        check_vma=False,
    )
```

```python
import functools

import jax
import jax.numpy as jnp
from jax import lax
from jax.experimental import pallas as pl
from jax.experimental.pallas import tpu as pltpu
from jax.sharding import PartitionSpec as P

F32 = jnp.float32
BF16 = jnp.bfloat16
MIB = 1024 * 1024
VMEM = pl.BlockSpec(memory_space=pltpu.VMEM)
ANY = pl.BlockSpec(memory_space=pl.ANY)
HBM = pl.BlockSpec(memory_space=pltpu.HBM)

ROWS = 2048
HALF = 1024
COLS = 896
RANK = 256
CHUNK = 256
BAND = 128
PART = 64
QUARTER = 32
BLOCK = 64
GROUP = 4


def split(value):
    high = value.astype(BF16)
    return high, (value - high.astype(F32)).astype(BF16)


def dot(left, right, contract):
    return lax.dot_general(left, right, (contract, ((), ())), preferred_element_type=F32)


def dot3(left, right, contract):
    (left_high, left_low), (right_high, right_low) = left, right
    return dot(left_high, right_high, contract) + (
        dot(left_high, right_low, contract) + dot(left_low, right_high, contract)
    )


NN = ((1,), (0,))
NT = ((1,), (1,))
TN = ((0,), (0,))


def call(kernel, outs, *args, specs=None, out_specs=None, scratch=(), limit=24):
    return pl.pallas_call(
        kernel,
        out_shape=[jax.ShapeDtypeStruct(shape, dtype) for shape, dtype in outs],
        in_specs=specs or [VMEM] * len(args),
        out_specs=out_specs or [VMEM] * len(outs),
        scratch_shapes=list(scratch),
        compiler_params=pltpu.CompilerParams(vmem_limit_bytes=limit * MIB),
    )(*args)


def here():
    col = lax.axis_index("col")
    return col & 1, (col >> 1) & 3, col >> 3, lax.axis_index("row")


def first_axis():
    core, x, y, _ = here()
    return jnp.where(core == 0, x, y)


def kept_half(level):
    core, _, _, z = here()
    if level == 0:
        return (z + core) & 1
    place = ((z >> 1) + core) & 3
    return ((place + 1) >> 1) & 1


def at(start, size, multiple):
    return pl.ds(pl.multiple_of(start, multiple), size)


PIECE = 256


def first_kernel(away, weight_ref, sketch_ref, out_ref, high_ref, low_ref):
    core = here()[0]
    half = 1 - core if away else core
    for i in range(HALF // PIECE):
        rows = slice(i * PIECE, (i + 1) * PIECE)
        high, low = split(weight_ref[at(half * HALF + i * PIECE, PIECE, PIECE), :])
        high_ref[rows, :] = high
        low_ref[rows, :] = low
        sketch = sketch_ref[...]
        out_ref[rows, :] = dot(high, sketch, NN) + dot(low, sketch, NN)


def first_product(away, weight, sketch):
    return call(
        functools.partial(first_kernel, away),
        [((HALF, RANK), F32), ((HALF, COLS), BF16), ((HALF, COLS), BF16)], weight, sketch,
    )


def swap(value):
    return lax.ppermute(value, "col", [(i, i ^ 1) for i in range(32)])


OTHERS = (1, 3, 2)


def permute_plane(value, flip, first):
    pairs = []
    for i in range(32):
        y, x, core = i // 8, (i // 2) % 4, i % 2
        if (core == 0) == first:
            x ^= flip
        else:
            y ^= flip
        pairs.append((i, y * 8 + x * 2 + core))
    return lax.ppermute(value, "col", pairs)


def exchange(own, pieces, first):
    return [own] + [permute_plane(p, flip, first) for flip, p in zip(OTHERS, pieces)]


def pieces_kernel(keep_ref, got_ref, *outs):
    for flip, out_ref in zip((0,) + OTHERS, outs):
        rows = at((first_axis() ^ flip) * CHUNK, CHUNK, CHUNK)
        out_ref[...] = keep_ref[rows, :] + got_ref[rows, :]


def sum_four(p0, p1, p3, p2):
    return (p0[...] + p2[...]) + (p1[...] + p3[...])


def sum_kernel(p0, p1, p3, p2, *outs):
    for out_ref in outs:
        out_ref[...] = sum_four(p0, p1, p3, p2)


def sum_turned_kernel(p0, p1, p3, p2, *outs):
    total = sum_four(p0, p1, p3, p2).T
    for out_ref in outs:
        out_ref[...] = total


def place_kernel(*refs):
    for flip, p in zip((0,) + OTHERS, refs):
        refs[-1][:, at((first_axis() ^ flip) * CHUNK, CHUNK, CHUNK)] = p[...]


def sum_col(keep, got):
    piece = ((CHUNK, RANK), F32)
    pieces = call(pieces_kernel, [piece] * 4, keep, got)
    last, *ones = call(sum_kernel, [piece] * 3, *exchange(pieces[0], pieces[1:], True))
    last, *ones = call(sum_turned_kernel, [piece] * 3, *exchange(last, ones + [last], False))
    pieces = exchange(last, ones + [last], True)
    return call(place_kernel, [((RANK, HALF), F32)], *pieces)[0]


def permute_halving(value, level):
    pairs = []
    for z in range(8):
        for i in range(32):
            core, place = i % 2, (z // 2 + i % 2) % 4
            if level == 0:
                other = z + 1 if z % 2 == core else z - 1
            else:
                partner = place ^ 1 if level == 1 else 3 - place
                other = (partner - core) % 4 * 2 + z % 2
            pairs.append((z * 32 + i, other % 8 * 32 + i))
    return lax.ppermute(value, ("row", "col"), pairs)


def halve(total, kept, size, send_ref, keep_ref):
    keep_ref[...] = total[at(kept * size, size, size), :]
    send_ref[...] = total[at((1 - kept) * size, size, size), :]


def back_own_kernel(turned_ref, high_ref, low_ref, out_ref):
    out_ref[...] = dot3(split(turned_ref[...]), (high_ref[...], low_ref[...]), NN)


def back_other_kernel(own_ref, turned_ref, high_ref, low_ref, out_ref):
    out_ref[...] = own_ref[...] + dot3(split(turned_ref[...]), (high_ref[...], low_ref[...]), NN)


def halve_first_kernel(total, _, send_ref, keep_ref):
    halve(total, kept_half(0), BAND, send_ref, keep_ref)


def halve_kernel(keep_ref, got_ref, _, send_out, keep_out, total):
    total[...] = keep_ref[...] + got_ref[...]
    halve(total, kept_half(1), PART, send_out, keep_out)


def add_kernel(left_ref, right_ref, *outs):
    for out_ref in outs:
        out_ref[...] = left_ref[...] + right_ref[...]


def add_after_kernel(left_ref, right_ref, _, out_ref):
    out_ref[...] = left_ref[...] + right_ref[...]


def join_kernel(keep_ref, got_ref, _, out_ref):
    kept = kept_half(1)
    out_ref[at(kept * PART, PART, PART), :] = keep_ref[...]
    out_ref[at((1 - kept) * PART, PART, PART), :] = got_ref[...]


def back_product(first, other, parts_other, side):
    whole, band, part = ((RANK, COLS), F32), ((BAND, COLS), F32), ((PART, COLS), F32)
    specs = [VMEM] * 2 + [ANY]
    total = call(back_other_kernel, [whole], first, other, *parts_other)[0]
    send, keep = call(halve_first_kernel, [band] * 2, total, side(total), specs=specs[1:])
    got = permute_halving(send, 0)
    send, keep = call(
        halve_kernel, [part] * 2, keep, got, side(None),
        specs=specs, scratch=[pltpu.VMEM((BAND, COLS), F32)],
    )
    got = permute_halving(send, 1)
    keep = call(add_after_kernel, [part], keep, got, side(None), specs=specs)[0]
    got = permute_halving(keep, 2)
    keep = call(add_after_kernel, [part], keep, got, side(None), specs=specs)[0]
    got = permute_halving(keep, 1)
    keep = call(join_kernel, [band], keep, got, side(None), specs=specs)[0]
    return keep, permute_halving(keep, 0)


def second_send_kernel(band, got, high_ref, low_ref, out_ref, turned_high, turned_low):
    kept = kept_half(0)
    for half, value in ((kept, band), (1 - kept, got)):
        rows = at(half * BAND, BAND, BAND)
        turned_high[rows, :], turned_low[rows, :] = split(value[...])
    out_ref[...] = dot3((high_ref[...], low_ref[...]), (turned_high[...], turned_low[...]), NT)


def second_keep_kernel(high_ref, low_ref, turned_high, turned_low, out_ref):
    out_ref[...] = dot3((high_ref[...], low_ref[...]), (turned_high[...], turned_low[...]), NT)


def gram_kernel(own_ref, send_ref, keep_ref):
    core, x, _, _ = here()
    kept = own_ref[at(core * BAND + x * QUARTER, QUARTER, QUARTER), :]
    sent = own_ref[at((1 - core) * BAND + x * QUARTER, QUARTER, QUARTER), :]
    both = jnp.concatenate([kept, sent], axis=0)
    product = dot3(split(both), split(own_ref[...]), NT)
    keep_ref[...] = product[:QUARTER, :]
    send_ref[...] = product[QUARTER:, :]


def place_gram_kernel(*refs):
    for flip, p in zip((0,) + OTHERS, refs):
        refs[-1][at((here()[1] ^ flip) * QUARTER, QUARTER, QUARTER), :] = p[...]


def permute_x(value, flip):
    return lax.ppermute(value, "col", [(i, i ^ (2 * flip)) for i in range(32)])


def gram_and_factor(own, other, results):
    piece = ((QUARTER, RANK), F32)
    send, keep = call(gram_kernel, [piece] * 2, own)
    one = call(add_kernel, [piece], keep, swap(send))[0]
    got = permute_halving(one, 0)
    after = yield
    one = call(add_after_kernel, [piece], one, got, after, specs=[VMEM] * 2 + [ANY])[0]
    yield one
    for level in (1, 2):
        got = permute_halving(one, level)
        ones = call(add_kernel, [piece] * (3 if level == 2 else 1), one, got)
        one = ones[0]
        yield one
    pieces = [one] + [permute_x(p, flip) for flip, p in zip(OTHERS, [*ones[1:], one])]
    half = call(
        place_gram_kernel, [((BAND, RANK), F32)], *pieces
    )[0]
    yield half
    wide = ((RANK, 2 * RANK), F32)
    half_done = call(
        factor_first_kernel, [wide], half, swap(half)
    )[0]
    yield half_done
    inverse = call(
        factor_last_kernel, [((RANK, RANK), BF16)] * 2, half_done,
        scratch=[pltpu.VMEM((RANK, 2 * RANK), F32)],
    )
    basis = ((ROWS, RANK), BF16)
    results += inverse + call(
        basis_kernel, [basis] * 3, own, other, *inverse
    )


def exact_dot(left, right, contract):
    return lax.dot_general(
        left, right, (contract, ((), ())), precision=lax.Precision.HIGHEST,
        preferred_element_type=F32,
    )


def eliminate(tile, start):
    row_of = lax.broadcasted_iota(jnp.int32, (BLOCK, 128), 0)
    for j in range(0, BLOCK, GROUP):
        columns = [
            jnp.broadcast_to(tile[:, start + j + m : start + j + m + 1], (BLOCK, 128))
            for m in range(GROUP)
        ]
        rows = [tile[j + m : j + m + 1, :] for m in range(GROUP)]
        scales = []
        for m in range(GROUP):
            pivot = columns[m][j + m : j + m + 1, :]
            inverse = 1.0 / pivot
            scales.append(lax.rsqrt(pivot))
            for n in range(m + 1, GROUP):
                rows[n] = rows[n] - rows[m] * (columns[m][j + n : j + n + 1, :] * inverse)
                columns[n] = columns[n] - columns[m] * (columns[n][j + m : j + m + 1, :] * inverse)
            columns[m] = jnp.where(row_of > j + m, columns[m], 0.0) * inverse
        for m in range(GROUP):
            tile = tile - columns[m] * rows[m]
        for m in range(GROUP):
            tile = jnp.where(row_of == j + m, rows[m] * scales[m], tile)
    return tile


def factor_block(work, k):
    row_of = lax.broadcasted_iota(jnp.int32, (BLOCK, 128), 0)
    lane_of = lax.broadcasted_iota(jnp.int32, (BLOCK, 128), 1)
    top = k * BLOCK
    base = top // 128 * 128
    start, other = top - base, BLOCK - (top - base)
    held = (lane_of >= start) & (lane_of < start + BLOCK)
    tile = work[top : top + BLOCK, base : base + 128]
    tile = jnp.where(held, tile, jnp.where(lane_of - other == row_of, 1.0, 0.0))
    tile = eliminate(tile, start)
    inverse = jnp.where(held, pltpu.roll(tile, 64, 1), 0.0)
    solved = exact_dot(inverse, work[base : base + 128, :], NN)
    work[top : top + BLOCK, :] = solved
    if top + BLOCK < RANK:
        update = exact_dot(solved[:, :RANK], solved, TN)
        work[top + BLOCK :, :] = work[top + BLOCK :, :] - update[top + BLOCK :, :]


def factor_first_kernel(half_ref, got_ref, work):
    core = here()[0]
    work[at(core * BAND, BAND, BAND), :RANK] = half_ref[...]
    work[at((1 - core) * BAND, BAND, BAND), :RANK] = got_ref[...]
    rows = lax.broadcasted_iota(jnp.int32, (RANK, RANK), 0)
    lanes = lax.broadcasted_iota(jnp.int32, (RANK, RANK), 1)
    work[:, RANK:] = jnp.where(rows == lanes, 1.0, 0.0)
    factor_block(work, 0)
    factor_block(work, 1)


def factor_last_kernel(half_done, inverse_high, inverse_low, work):
    work[...] = half_done[...]
    factor_block(work, 2)
    factor_block(work, 3)
    inverse_high[...], inverse_low[...] = split(work[:, RANK:])


def basis_kernel(own_ref, other_ref, inverse_high, inverse_low, left_ref, high_ref, low_ref):
    inverse = inverse_high[...], inverse_low[...]
    for half, ref in ((here()[0], own_ref), (1 - here()[0], other_ref)):
        for k in range(HALF // 256):
            rows = at(half * HALF + k * 256, 256, 256)
            orthonormal = dot3(split(ref[:, k * 256 : (k + 1) * 256].T), inverse, NT)
            left_ref[rows, :] = (64.0 * orthonormal).astype(BF16)
            high_ref[rows, :], low_ref[rows, :] = split(orthonormal)


STEP = 256


def last_kernel(
    own_high, own_low, other_high, other_low, basis_high, basis_low, inverse_high, inverse_low,
    band, got, residual_ref, right_ref, z_work, c_high, c_low, held, sems
):
    core, kept = here()[0], kept_half(0)
    z_work[at(kept * BAND, BAND, BAND), :] = band[...]
    z_work[at((1 - kept) * BAND, BAND, BAND), :] = got[...]
    coefficient = dot3((inverse_high[...], inverse_low[...]), split(z_work[...]), NN)
    right_ref[...] = (coefficient * (1.0 / 64.0)).astype(BF16)
    c_high[...], c_low[...] = split(coefficient)
    stacked = jnp.concatenate([c_high[...], c_high[...], c_low[...]], axis=0)
    copies = []
    for half, high, low in ((core, own_high, own_low), (1 - core, other_high, other_low)):
        for k in range(HALF // STEP):
            rows = at(half * HALF + k * STEP, STEP, STEP)
            here_rows = slice(k * STEP, (k + 1) * STEP)
            slot = held.at[len(copies)]
            first, second = basis_high[rows, :], basis_low[rows, :]
            product = dot(jnp.concatenate([first, second, first], axis=1), stacked, NN)
            weight = high[here_rows, :].astype(F32) + low[here_rows, :].astype(F32)
            slot[...] = (weight - product).astype(BF16)
            copies.append(
                pltpu.make_async_copy(slot, residual_ref.at[rows, :], sems.at[len(copies)])
            )
            copies[-1].start()
    for copy in copies:
        copy.wait()


def last_product(parts_own, parts_other, basis, inverse, band, got):
    steps = ROWS // STEP
    return call(
        last_kernel, [((ROWS, COLS), BF16), ((RANK, COLS), BF16)],
        *parts_own, *parts_other, *basis, *inverse, band, got,
        out_specs=[HBM, VMEM],
        scratch=[
            pltpu.VMEM((RANK, COLS), F32), pltpu.VMEM((RANK, COLS), BF16),
            pltpu.VMEM((RANK, COLS), BF16), pltpu.VMEM((steps, STEP, COLS), BF16),
            pltpu.SemaphoreType.DMA((steps,)),
        ],
    )


def per_device(weight, sketch):
    send, *parts_other = first_product(True, weight, sketch)
    got = swap(send)
    keep, *parts_own = first_product(False, weight, sketch)
    own = sum_col(keep, got)
    other = swap(own)
    first = call(back_own_kernel, [((RANK, COLS), F32)], own, *parts_own)[0]
    bands = back_product(first, other, parts_other, lambda _: first)

    turned = ((RANK, COLS), BF16)
    send, *projected = call(
        second_send_kernel, [((HALF, RANK), F32), turned, turned], *bands, *parts_other
    )
    got = swap(send)
    keep = call(second_keep_kernel, [((HALF, RANK), F32)], *parts_own, *projected)[0]
    own = sum_col(keep, got)
    other = swap(own)
    first = call(back_own_kernel, [((RANK, COLS), F32)], own, *parts_own)[0]
    results = []
    side = gram_and_factor(own, other, results)
    next(side)
    bands = back_product(first, other, parts_other, side.send)
    next(side, None)
    inverse, left_adapter, basis = results[:2], results[2], results[3:]
    residual, right_adapter = last_product(
        parts_own, parts_other, basis, inverse, *bands
    )
    return residual, left_adapter, right_adapter


def solution(mesh):
    return jax.shard_map(
        per_device,
        mesh=mesh,
        in_specs=(P("row", "col"), P("col", None)),
        out_specs=(P("row", "col"), P("row", None), P(None, "col")),
        check_vma=False,
    )
```

```python
import functools

import jax
import jax.numpy as jnp
from jax import lax
from jax.experimental import pallas as pl
from jax.experimental.pallas import tpu as pltpu
from jax.sharding import PartitionSpec as P

F32 = jnp.float32
BF16 = jnp.bfloat16
MIB = 1024 * 1024
VMEM = pl.BlockSpec(memory_space=pltpu.VMEM)
ANY = pl.BlockSpec(memory_space=pl.ANY)
HBM = pl.BlockSpec(memory_space=pltpu.HBM)

ROWS = 2048
HALF = 1024
COLS = 896
RANK = 256
CHUNK = 256
BAND = 128
PART = 64
QUARTER = 32
BLOCK = 64
GROUP = 4


def split(value):
    high = value.astype(BF16)
    return high, (value - high.astype(F32)).astype(BF16)


def dot(left, right, contract):
    return lax.dot_general(left, right, (contract, ((), ())), preferred_element_type=F32)


def dot3(left, right, contract):
    (left_high, left_low), (right_high, right_low) = left, right
    return dot(left_high, right_high, contract) + (
        dot(left_high, right_low, contract) + dot(left_low, right_high, contract)
    )


NN = ((1,), (0,))
NT = ((1,), (1,))
TN = ((0,), (0,))


def call(kernel, outs, *args, specs=None, out_specs=None, scratch=(), limit=24):
    return pl.pallas_call(
        kernel,
        out_shape=[jax.ShapeDtypeStruct(shape, dtype) for shape, dtype in outs],
        in_specs=specs or [VMEM] * len(args),
        out_specs=out_specs or [VMEM] * len(outs),
        scratch_shapes=list(scratch),
        compiler_params=pltpu.CompilerParams(vmem_limit_bytes=limit * MIB),
    )(*args)


def here():
    col = lax.axis_index("col")
    return col & 1, (col >> 1) & 3, col >> 3, lax.axis_index("row")


def first_axis():
    core, x, y, _ = here()
    return jnp.where(core == 0, x, y)


def kept_half(level, near):
    core, _, _, z = here()
    if near:
        turn = (z - core) & 7
        return ((turn + 1) >> 1) & 1 if level == 0 else (jnp.int32(0b10110100) >> turn) & 1
    if level == 0:
        return (z + core) & 1
    place = ((z >> 1) + core) & 3
    return ((place + 1) >> 1) & 1


def at(start, size, multiple):
    return pl.ds(pl.multiple_of(start, multiple), size)


PIECE = 256


def first_kernel(away, weight_ref, sketch_ref, out_ref, high_ref, low_ref):
    core = here()[0]
    half = 1 - core if away else core
    for i in range(HALF // PIECE):
        rows = slice(i * PIECE, (i + 1) * PIECE)
        high, low = split(weight_ref[at(half * HALF + i * PIECE, PIECE, PIECE), :])
        high_ref[rows, :] = high
        low_ref[rows, :] = low
        sketch = sketch_ref[...]
        out_ref[rows, :] = dot(high, sketch, NN) + dot(low, sketch, NN)


def first_product(away, weight, sketch):
    return call(
        functools.partial(first_kernel, away),
        [((HALF, RANK), F32), ((HALF, COLS), BF16), ((HALF, COLS), BF16)], weight, sketch,
    )


def swap(value):
    return lax.ppermute(value, "col", [(i, i ^ 1) for i in range(32)])


OTHERS = (1, 3, 2)


def permute_plane(value, flip, first):
    pairs = []
    for i in range(32):
        y, x, core = i // 8, (i // 2) % 4, i % 2
        if (core == 0) == first:
            x ^= flip
        else:
            y ^= flip
        pairs.append((i, y * 8 + x * 2 + core))
    return lax.ppermute(value, "col", pairs)


def exchange(own, pieces, first):
    return [own] + [permute_plane(p, flip, first) for flip, p in zip(OTHERS, pieces)]


def pieces_kernel(keep_ref, got_ref, *outs):
    for flip, out_ref in zip((0,) + OTHERS, outs):
        rows = at((first_axis() ^ flip) * CHUNK, CHUNK, CHUNK)
        out_ref[...] = keep_ref[rows, :] + got_ref[rows, :]


def sum_four(p0, p1, p3, p2):
    return (p0[...] + p2[...]) + (p1[...] + p3[...])


def sum_kernel(p0, p1, p3, p2, *outs):
    for out_ref in outs:
        out_ref[...] = sum_four(p0, p1, p3, p2)


def sum_turned_kernel(p0, p1, p3, p2, *outs):
    total = sum_four(p0, p1, p3, p2).T
    for out_ref in outs:
        out_ref[...] = total


def place_kernel(*refs):
    for flip, p in zip((0,) + OTHERS, refs):
        refs[-1][:, at((first_axis() ^ flip) * CHUNK, CHUNK, CHUNK)] = p[...]


def sum_col(keep, got):
    piece = ((CHUNK, RANK), F32)
    pieces = call(pieces_kernel, [piece] * 4, keep, got)
    last, *ones = call(sum_kernel, [piece] * 3, *exchange(pieces[0], pieces[1:], True))
    last, *ones = call(sum_turned_kernel, [piece] * 3, *exchange(last, ones + [last], False))
    pieces = exchange(last, ones + [last], True)
    return call(place_kernel, [((RANK, HALF), F32)], *pieces)[0]


def permute_z(value, partner):
    pairs = [(z * 32 + i, partner(z, i % 2) % 8 * 32 + i) for z in range(8) for i in range(32)]
    return lax.ppermute(value, ("row", "col"), pairs)


def permute_near(value, level):
    def partner(z, core):
        turn = (z - core) % 8
        if level == 0:
            turn ^= 1
        elif level == 1:
            turn += 1 if turn % 2 else -1
        else:
            turn = (7 if turn in (1, 2, 5, 6) else 3) - turn
        return turn + core

    return permute_z(value, partner)


def permute_parity(value, level):
    def partner(z, core):
        place = (z // 2 + core) % 4
        if level == 0:
            return z + 1 if z % 2 == core else z - 1
        return ((place ^ 1 if level == 1 else 3 - place) - core) % 4 * 2 + z % 2

    return permute_z(value, partner)


def halve(total, kept, size, send_ref, keep_ref):
    keep_ref[...] = total[at(kept * size, size, size), :]
    send_ref[...] = total[at((1 - kept) * size, size, size), :]


def back_own_kernel(turned_ref, high_ref, low_ref, out_ref):
    out_ref[...] = dot3(split(turned_ref[...]), (high_ref[...], low_ref[...]), NN)


def back_other_kernel(own_ref, turned_ref, high_ref, low_ref, out_ref):
    out_ref[...] = own_ref[...] + dot3(split(turned_ref[...]), (high_ref[...], low_ref[...]), NN)


def halve_first_kernel(near, total, _, send_ref, keep_ref):
    halve(total, kept_half(0, near), BAND, send_ref, keep_ref)


def halve_kernel(near, keep_ref, got_ref, _, send_out, keep_out, total):
    total[...] = keep_ref[...] + got_ref[...]
    halve(total, kept_half(1, near), PART, send_out, keep_out)


def add_kernel(left_ref, right_ref, *outs):
    for out_ref in outs:
        out_ref[...] = left_ref[...] + right_ref[...]


def add_after_kernel(left_ref, right_ref, _, out_ref):
    out_ref[...] = left_ref[...] + right_ref[...]


def join_kernel(near, keep_ref, got_ref, _, out_ref):
    kept = kept_half(1, near)
    out_ref[at(kept * PART, PART, PART), :] = keep_ref[...]
    out_ref[at((1 - kept) * PART, PART, PART), :] = got_ref[...]


def back_product(first, other, parts_other, near, side):
    permute = permute_near if near else permute_parity
    whole, band, part = ((RANK, COLS), F32), ((BAND, COLS), F32), ((PART, COLS), F32)
    specs = [VMEM] * 2 + [ANY]
    total = call(back_other_kernel, [whole], first, other, *parts_other)[0]
    send, keep = call(
        functools.partial(halve_first_kernel, near), [band] * 2, total, side(total), specs=specs[1:])
    got = permute(send, 0)
    send, keep = call(
        functools.partial(halve_kernel, near), [part] * 2, keep, got, side(None),
        specs=specs, scratch=[pltpu.VMEM((BAND, COLS), F32)],
    )
    got = permute(send, 1)
    keep = call(add_after_kernel, [part], keep, got, side(None), specs=specs)[0]
    got = permute(keep, 2)
    keep = call(add_after_kernel, [part], keep, got, side(None), specs=specs)[0]
    got = permute(keep, 1)
    keep = call(functools.partial(join_kernel, near), [band], keep, got, side(None), specs=specs)[0]
    return keep, permute(keep, 0)


def second_send_kernel(band, got, high_ref, low_ref, out_ref, turned_high, turned_low):
    kept = kept_half(0, True)
    for half, value in ((kept, band), (1 - kept, got)):
        rows = at(half * BAND, BAND, BAND)
        turned_high[rows, :], turned_low[rows, :] = split(value[...])
    out_ref[...] = dot3((high_ref[...], low_ref[...]), (turned_high[...], turned_low[...]), NT)


def second_keep_kernel(high_ref, low_ref, turned_high, turned_low, out_ref):
    out_ref[...] = dot3((high_ref[...], low_ref[...]), (turned_high[...], turned_low[...]), NT)


def gram_kernel(own_ref, send_ref, keep_ref):
    core, x, _, _ = here()
    kept = own_ref[at(core * BAND + x * QUARTER, QUARTER, QUARTER), :]
    sent = own_ref[at((1 - core) * BAND + x * QUARTER, QUARTER, QUARTER), :]
    both = jnp.concatenate([kept, sent], axis=0)
    product = dot3(split(both), split(own_ref[...]), NT)
    keep_ref[...] = product[:QUARTER, :]
    send_ref[...] = product[QUARTER:, :]


def place_gram_kernel(*refs):
    for flip, p in zip((0,) + OTHERS, refs):
        refs[-1][at((here()[1] ^ flip) * QUARTER, QUARTER, QUARTER), :] = p[...]


def permute_x(value, flip):
    return lax.ppermute(value, "col", [(i, i ^ (2 * flip)) for i in range(32)])


def gram_and_factor(own, other, results):
    piece = ((QUARTER, RANK), F32)
    send, keep = call(gram_kernel, [piece] * 2, own)
    one = call(add_kernel, [piece], keep, swap(send))[0]
    got = permute_parity(one, 0)
    after = yield
    one = call(add_after_kernel, [piece], one, got, after, specs=[VMEM] * 2 + [ANY])[0]
    yield one
    for level in (1, 2):
        got = permute_parity(one, level)
        ones = call(add_kernel, [piece] * (3 if level == 2 else 1), one, got)
        one = ones[0]
        yield one
    pieces = [one] + [permute_x(p, flip) for flip, p in zip(OTHERS, [*ones[1:], one])]
    half = call(
        place_gram_kernel, [((BAND, RANK), F32)], *pieces
    )[0]
    yield half
    wide = ((RANK, 2 * RANK), F32)
    half_done = call(
        factor_first_kernel, [wide], half, swap(half)
    )[0]
    yield half_done
    inverse = call(
        factor_last_kernel, [((RANK, RANK), BF16)] * 2, half_done,
        scratch=[pltpu.VMEM((RANK, 2 * RANK), F32)],
    )
    basis = ((ROWS, RANK), BF16)
    results += inverse + call(
        basis_kernel, [basis] * 3, own, other, *inverse
    )


def exact_dot(left, right, contract):
    return lax.dot_general(
        left, right, (contract, ((), ())), precision=lax.Precision.HIGHEST,
        preferred_element_type=F32,
    )


def eliminate(tile, start):
    row_of = lax.broadcasted_iota(jnp.int32, (BLOCK, 128), 0)
    for j in range(0, BLOCK, GROUP):
        columns = [
            jnp.broadcast_to(tile[:, start + j + m : start + j + m + 1], (BLOCK, 128))
            for m in range(GROUP)
        ]
        rows = [tile[j + m : j + m + 1, :] for m in range(GROUP)]
        scales = []
        for m in range(GROUP):
            pivot = columns[m][j + m : j + m + 1, :]
            inverse = 1.0 / pivot
            scales.append(lax.rsqrt(pivot))
            for n in range(m + 1, GROUP):
                rows[n] = rows[n] - rows[m] * (columns[m][j + n : j + n + 1, :] * inverse)
                columns[n] = columns[n] - columns[m] * (columns[n][j + m : j + m + 1, :] * inverse)
            columns[m] = jnp.where(row_of > j + m, columns[m], 0.0) * inverse
        for m in range(GROUP):
            tile = tile - columns[m] * rows[m]
        for m in range(GROUP):
            tile = jnp.where(row_of == j + m, rows[m] * scales[m], tile)
    return tile


def factor_block(work, k):
    row_of = lax.broadcasted_iota(jnp.int32, (BLOCK, 128), 0)
    lane_of = lax.broadcasted_iota(jnp.int32, (BLOCK, 128), 1)
    top = k * BLOCK
    base = top // 128 * 128
    start, other = top - base, BLOCK - (top - base)
    held = (lane_of >= start) & (lane_of < start + BLOCK)
    tile = work[top : top + BLOCK, base : base + 128]
    tile = jnp.where(held, tile, jnp.where(lane_of - other == row_of, 1.0, 0.0))
    tile = eliminate(tile, start)
    inverse = jnp.where(held, pltpu.roll(tile, 64, 1), 0.0)
    solved = exact_dot(inverse, work[base : base + 128, :], NN)
    work[top : top + BLOCK, :] = solved
    if top + BLOCK < RANK:
        update = exact_dot(solved[:, :RANK], solved, TN)
        work[top + BLOCK :, :] = work[top + BLOCK :, :] - update[top + BLOCK :, :]


def factor_first_kernel(half_ref, got_ref, work):
    core = here()[0]
    work[at(core * BAND, BAND, BAND), :RANK] = half_ref[...]
    work[at((1 - core) * BAND, BAND, BAND), :RANK] = got_ref[...]
    rows = lax.broadcasted_iota(jnp.int32, (RANK, RANK), 0)
    lanes = lax.broadcasted_iota(jnp.int32, (RANK, RANK), 1)
    work[:, RANK:] = jnp.where(rows == lanes, 1.0, 0.0)
    factor_block(work, 0)
    factor_block(work, 1)


def factor_last_kernel(half_done, inverse_high, inverse_low, work):
    work[...] = half_done[...]
    factor_block(work, 2)
    factor_block(work, 3)
    inverse_high[...], inverse_low[...] = split(work[:, RANK:])


def basis_kernel(own_ref, other_ref, inverse_high, inverse_low, left_ref, high_ref, low_ref):
    inverse = inverse_high[...], inverse_low[...]
    for half, ref in ((here()[0], own_ref), (1 - here()[0], other_ref)):
        for k in range(HALF // 256):
            rows = at(half * HALF + k * 256, 256, 256)
            orthonormal = dot3(split(ref[:, k * 256 : (k + 1) * 256].T), inverse, NT)
            left_ref[rows, :] = (64.0 * orthonormal).astype(BF16)
            high_ref[rows, :], low_ref[rows, :] = split(orthonormal)


STEP = 256


def last_kernel(
    own_high, own_low, other_high, other_low, basis_high, basis_low, inverse_high, inverse_low,
    band, got, residual_ref, right_out, z_work, c_high, c_low, right_ref, held, sems
):
    core, kept = here()[0], kept_half(0, False)
    z_work[at(kept * BAND, BAND, BAND), :] = band[...]
    z_work[at((1 - kept) * BAND, BAND, BAND), :] = got[...]
    coefficient = dot3((inverse_high[...], inverse_low[...]), split(z_work[...]), NN)
    right_ref[...] = (coefficient * (1.0 / 64.0)).astype(BF16)
    right_copy = pltpu.make_async_copy(right_ref, right_out, sems.at[ROWS // STEP])
    right_copy.start()
    c_high[...], c_low[...] = split(coefficient)
    stacked = jnp.concatenate([c_high[...], c_high[...], c_low[...]], axis=0)
    copies = []
    for half, high, low in ((core, own_high, own_low), (1 - core, other_high, other_low)):
        for k in range(HALF // STEP):
            rows = at(half * HALF + k * STEP, STEP, STEP)
            here_rows = slice(k * STEP, (k + 1) * STEP)
            slot = held.at[len(copies)]
            first, second = basis_high[rows, :], basis_low[rows, :]
            product = dot(jnp.concatenate([first, second, first], axis=1), stacked, NN)
            weight = high[here_rows, :].astype(F32) + low[here_rows, :].astype(F32)
            slot[...] = (weight - product).astype(BF16)
            copies.append(
                pltpu.make_async_copy(slot, residual_ref.at[rows, :], sems.at[len(copies)])
            )
            copies[-1].start()
    for copy in copies + [right_copy]:
        copy.wait()


def last_product(parts_own, parts_other, basis, inverse, band, got):
    steps = ROWS // STEP
    return call(
        last_kernel, [((ROWS, COLS), BF16), ((RANK, COLS), BF16)],
        *parts_own, *parts_other, *basis, *inverse, band, got,
        out_specs=[HBM, HBM],
        scratch=[
            pltpu.VMEM((RANK, COLS), F32), pltpu.VMEM((RANK, COLS), BF16),
            pltpu.VMEM((RANK, COLS), BF16), pltpu.VMEM((RANK, COLS), BF16),
            pltpu.VMEM((steps, STEP, COLS), BF16), pltpu.SemaphoreType.DMA((steps + 1,)),
        ],
    )


def per_device(weight, sketch):
    send, *parts_other = first_product(True, weight, sketch)
    got = swap(send)
    keep, *parts_own = first_product(False, weight, sketch)
    own = sum_col(keep, got)
    other = swap(own)
    first = call(back_own_kernel, [((RANK, COLS), F32)], own, *parts_own)[0]
    bands = back_product(first, other, parts_other, True, lambda _: first)

    turned = ((RANK, COLS), BF16)
    send, *projected = call(
        second_send_kernel, [((HALF, RANK), F32), turned, turned], *bands, *parts_other
    )
    got = swap(send)
    keep = call(second_keep_kernel, [((HALF, RANK), F32)], *parts_own, *projected)[0]
    own = sum_col(keep, got)
    other = swap(own)
    first = call(back_own_kernel, [((RANK, COLS), F32)], own, *parts_own)[0]
    results = []
    side = gram_and_factor(own, other, results)
    next(side)
    bands = back_product(first, other, parts_other, False, side.send)
    next(side, None)
    inverse, left_adapter, basis = results[:2], results[2], results[3:]
    residual, right_adapter = last_product(
        parts_own, parts_other, basis, inverse, *bands
    )
    return residual, left_adapter, right_adapter


def solution(mesh):
    return jax.shard_map(
        per_device,
        mesh=mesh,
        in_specs=(P("row", "col"), P("col", None)),
        out_specs=(P("row", "col"), P("row", None), P(None, "col")),
        check_vma=False,
    )
```

```python
import functools

import jax
import jax.numpy as jnp
from jax import lax
from jax.experimental import pallas as pl
from jax.experimental.pallas import tpu as pltpu
from jax.sharding import PartitionSpec as P

F32 = jnp.float32
BF16 = jnp.bfloat16
MIB = 1024 * 1024
VMEM = pl.BlockSpec(memory_space=pltpu.VMEM)
ANY = pl.BlockSpec(memory_space=pl.ANY)
HBM = pl.BlockSpec(memory_space=pltpu.HBM)

ROWS = 2048
HALF = 1024
COLS = 896
RANK = 256
CHUNK = 256
BAND = 128
PART = 64
QUARTER = 32
BLOCK = 64
GROUP = 4


def split(value):
    high = value.astype(BF16)
    return high, (value - high.astype(F32)).astype(BF16)


def dot(left, right, contract):
    return lax.dot_general(left, right, (contract, ((), ())), preferred_element_type=F32)


def dot3(left, right, contract):
    (left_high, left_low), (right_high, right_low) = left, right
    return dot(left_high, right_high, contract) + (
        dot(left_high, right_low, contract) + dot(left_low, right_high, contract)
    )


NN = ((1,), (0,))
NT = ((1,), (1,))
TN = ((0,), (0,))


def call(kernel, outs, *args, specs=None, out_specs=None, scratch=(), limit=24):
    return pl.pallas_call(
        kernel,
        out_shape=[jax.ShapeDtypeStruct(shape, dtype) for shape, dtype in outs],
        in_specs=specs or [VMEM] * len(args),
        out_specs=out_specs or [VMEM] * len(outs),
        scratch_shapes=list(scratch),
        compiler_params=pltpu.CompilerParams(vmem_limit_bytes=limit * MIB),
    )(*args)


def here():
    col = lax.axis_index("col")
    return col & 1, (col >> 1) & 3, col >> 3, lax.axis_index("row")


def first_axis():
    core, x, y, _ = here()
    return jnp.where(core == 0, x, y)


def kept_half(level, near):
    core, _, _, z = here()
    if near:
        turn = (z - core) & 7
        return ((turn + 1) >> 1) & 1 if level == 0 else (jnp.int32(0b10110100) >> turn) & 1
    if level == 0:
        return (z + core) & 1
    place = ((z >> 1) + core) & 3
    return ((place + 1) >> 1) & 1


def at(start, size, multiple):
    return pl.ds(pl.multiple_of(start, multiple), size)


PIECE = 256


def first_kernel(away, weight_ref, sketch_ref, out_ref, high_ref, low_ref):
    core = here()[0]
    half = 1 - core if away else core
    for i in range(HALF // PIECE):
        rows = slice(i * PIECE, (i + 1) * PIECE)
        high, low = split(weight_ref[at(half * HALF + i * PIECE, PIECE, PIECE), :])
        high_ref[rows, :] = high
        low_ref[rows, :] = low
        sketch = sketch_ref[...]
        out_ref[rows, :] = dot(high, sketch, NN) + dot(low, sketch, NN)


def first_product(away, weight, sketch):
    return call(
        functools.partial(first_kernel, away),
        [((HALF, RANK), F32), ((HALF, COLS), BF16), ((HALF, COLS), BF16)], weight, sketch,
    )


def swap(value):
    return lax.ppermute(value, "col", [(i, i ^ 1) for i in range(32)])


OTHERS = (1, 3, 2)


def permute_plane(value, flip, first):
    pairs = []
    for i in range(32):
        y, x, core = i // 8, (i // 2) % 4, i % 2
        if (core == 0) == first:
            x ^= flip
        else:
            y ^= flip
        pairs.append((i, y * 8 + x * 2 + core))
    return lax.ppermute(value, "col", pairs)


def exchange(own, pieces, first):
    return [own] + [permute_plane(p, flip, first) for flip, p in zip(OTHERS, pieces)]


def pieces_kernel(keep_ref, got_ref, *outs):
    for flip, out_ref in zip((0,) + OTHERS, outs):
        rows = at((first_axis() ^ flip) * CHUNK, CHUNK, CHUNK)
        out_ref[...] = keep_ref[rows, :] + got_ref[rows, :]


def sum_four(p0, p1, p3, p2):
    return (p0[...] + p2[...]) + (p1[...] + p3[...])


def sum_kernel(p0, p1, p3, p2, *outs):
    for out_ref in outs:
        out_ref[...] = sum_four(p0, p1, p3, p2)


def sum_turned_kernel(p0, p1, p3, p2, *outs):
    total = sum_four(p0, p1, p3, p2).T
    for out_ref in outs:
        out_ref[...] = total


def place_kernel(*refs):
    for flip, p in zip((0,) + OTHERS, refs):
        refs[-1][:, at((first_axis() ^ flip) * CHUNK, CHUNK, CHUNK)] = p[...]


def sum_col(keep, got):
    piece = ((CHUNK, RANK), F32)
    pieces = call(pieces_kernel, [piece] * 4, keep, got)
    last, *ones = call(sum_kernel, [piece] * 3, *exchange(pieces[0], pieces[1:], True))
    last, *ones = call(sum_turned_kernel, [piece] * 3, *exchange(last, ones + [last], False))
    pieces = exchange(last, ones + [last], True)
    return call(place_kernel, [((RANK, HALF), F32)], *pieces)[0]


def permute_z(value, partner):
    pairs = [(z * 32 + i, partner(z, i % 2) % 8 * 32 + i) for z in range(8) for i in range(32)]
    return lax.ppermute(value, ("row", "col"), pairs)


def permute_near(value, level):
    def partner(z, core):
        turn = (z - core) % 8
        if level == 0:
            turn ^= 1
        elif level == 1:
            turn += 1 if turn % 2 else -1
        else:
            turn = (7 if turn in (1, 2, 5, 6) else 3) - turn
        return turn + core

    return permute_z(value, partner)


def permute_parity(value, level):
    def partner(z, core):
        place = (z // 2 + core) % 4
        if level == 0:
            return z + 1 if z % 2 == core else z - 1
        return ((place ^ 1 if level == 1 else 3 - place) - core) % 4 * 2 + z % 2

    return permute_z(value, partner)


def halve(total, kept, size, send_ref, keep_ref):
    keep_ref[...] = total[at(kept * size, size, size), :]
    send_ref[...] = total[at((1 - kept) * size, size, size), :]


def back_own_kernel(turned_ref, high_ref, low_ref, out_ref):
    out_ref[...] = dot3(split(turned_ref[...]), (high_ref[...], low_ref[...]), NN)


def back_other_kernel(own_ref, turned_ref, high_ref, low_ref, out_ref):
    out_ref[...] = own_ref[...] + dot3(split(turned_ref[...]), (high_ref[...], low_ref[...]), NN)


def halve_first_kernel(near, total, _, send_ref, keep_ref):
    halve(total, kept_half(0, near), BAND, send_ref, keep_ref)


def halve_kernel(near, keep_ref, got_ref, _, send_out, keep_out, total):
    total[...] = keep_ref[...] + got_ref[...]
    halve(total, kept_half(1, near), PART, send_out, keep_out)


def add_kernel(left_ref, right_ref, *outs):
    for out_ref in outs:
        out_ref[...] = left_ref[...] + right_ref[...]


def add_after_kernel(left_ref, right_ref, _, out_ref):
    out_ref[...] = left_ref[...] + right_ref[...]


def join_kernel(near, keep_ref, got_ref, _, out_ref):
    kept = kept_half(1, near)
    out_ref[at(kept * PART, PART, PART), :] = keep_ref[...]
    out_ref[at((1 - kept) * PART, PART, PART), :] = got_ref[...]


def back_product(first, other, parts_other, near, side):
    permute = permute_near if near else permute_parity
    whole, band, part = ((RANK, COLS), F32), ((BAND, COLS), F32), ((PART, COLS), F32)
    specs = [VMEM] * 2 + [ANY]
    total = call(back_other_kernel, [whole], first, other, *parts_other)[0]
    send, keep = call(
        functools.partial(halve_first_kernel, near), [band] * 2, total, side(total), specs=specs[1:])
    got = permute(send, 0)
    send, keep = call(
        functools.partial(halve_kernel, near), [part] * 2, keep, got, side(None),
        specs=specs, scratch=[pltpu.VMEM((BAND, COLS), F32)],
    )
    got = permute(send, 1)
    keep = call(add_after_kernel, [part], keep, got, side(None), specs=specs)[0]
    got = permute(keep, 2)
    keep = call(add_after_kernel, [part], keep, got, side(None), specs=specs)[0]
    got = permute(keep, 1)
    keep = call(functools.partial(join_kernel, near), [band], keep, got, side(None), specs=specs)[0]
    return keep, permute(keep, 0)


def second_send_kernel(band, got, high_ref, low_ref, out_ref, turned_high, turned_low):
    kept = kept_half(0, True)
    for half, value in ((kept, band), (1 - kept, got)):
        rows = at(half * BAND, BAND, BAND)
        turned_high[rows, :], turned_low[rows, :] = split(value[...])
    out_ref[...] = dot3((high_ref[...], low_ref[...]), (turned_high[...], turned_low[...]), NT)


def second_keep_kernel(high_ref, low_ref, turned_high, turned_low, out_ref):
    out_ref[...] = dot3((high_ref[...], low_ref[...]), (turned_high[...], turned_low[...]), NT)


def gram_kernel(own_ref, out_ref):
    core, x, _, _ = here()
    kept = own_ref[at(core * BAND + x * QUARTER, QUARTER, QUARTER), :]
    sent = own_ref[at((1 - core) * BAND + x * QUARTER, QUARTER, QUARTER), :]
    both = jnp.concatenate([kept, sent], axis=0)
    out_ref[...] = dot3(split(both), split(own_ref[...]), NT)


def gram_pair_kernel(left_ref, right_ref, _, keep_ref, send_ref):
    keep_ref[...] = left_ref[:QUARTER, :] + right_ref[:QUARTER, :]
    send_ref[...] = left_ref[QUARTER:, :] + right_ref[QUARTER:, :]


def place_gram_kernel(*refs):
    for flip, p in zip((0,) + OTHERS, refs):
        refs[-1][at((here()[1] ^ flip) * QUARTER, QUARTER, QUARTER), :] = p[...]


def permute_x(value, flip):
    return lax.ppermute(value, "col", [(i, i ^ (2 * flip)) for i in range(32)])


def gram_and_factor(own, other, results):
    piece = ((QUARTER, RANK), F32)
    both = call(gram_kernel, [((2 * QUARTER, RANK), F32)], own)[0]
    got = permute_z(both, lambda z, core: z ^ 1)
    after = yield
    specs = [VMEM] * 2 + [ANY]
    keep, send = call(gram_pair_kernel, [piece] * 2, both, got, after, specs=specs)
    yield keep
    one = call(add_kernel, [piece], keep, swap(send))[0]
    for level in (1, 2):
        got = permute_parity(one, level)
        ones = call(add_kernel, [piece] * (3 if level == 2 else 1), one, got)
        one = ones[0]
        yield one
    pieces = [one] + [permute_x(p, flip) for flip, p in zip(OTHERS, [*ones[1:], one])]
    half = call(
        place_gram_kernel, [((BAND, RANK), F32)], *pieces
    )[0]
    yield half
    wide = ((RANK, 2 * RANK), F32)
    half_done = call(
        factor_first_kernel, [wide], half, swap(half)
    )[0]
    yield half_done
    inverse = call(
        factor_last_kernel, [((RANK, RANK), BF16)] * 2, half_done,
        scratch=[pltpu.VMEM((RANK, 2 * RANK), F32)],
    )
    basis = ((ROWS, RANK), BF16)
    results += inverse + call(
        basis_kernel, [basis] * 3, own, other, *inverse
    )


def exact_dot(left, right, contract):
    return lax.dot_general(
        left, right, (contract, ((), ())), precision=lax.Precision.HIGHEST,
        preferred_element_type=F32,
    )


def eliminate(tile, start):
    row_of = lax.broadcasted_iota(jnp.int32, (BLOCK, 128), 0)
    for j in range(0, BLOCK, GROUP):
        columns = [
            jnp.broadcast_to(tile[:, start + j + m : start + j + m + 1], (BLOCK, 128))
            for m in range(GROUP)
        ]
        rows = [tile[j + m : j + m + 1, :] for m in range(GROUP)]
        scales = []
        for m in range(GROUP):
            pivot = columns[m][j + m : j + m + 1, :]
            inverse = 1.0 / pivot
            scales.append(lax.rsqrt(pivot))
            for n in range(m + 1, GROUP):
                rows[n] = rows[n] - rows[m] * (columns[m][j + n : j + n + 1, :] * inverse)
                columns[n] = columns[n] - columns[m] * (columns[n][j + m : j + m + 1, :] * inverse)
            columns[m] = jnp.where(row_of > j + m, columns[m], 0.0) * inverse
        for m in range(GROUP):
            tile = tile - columns[m] * rows[m]
        for m in range(GROUP):
            tile = jnp.where(row_of == j + m, rows[m] * scales[m], tile)
    return tile


def factor_block(work, k):
    row_of = lax.broadcasted_iota(jnp.int32, (BLOCK, 128), 0)
    lane_of = lax.broadcasted_iota(jnp.int32, (BLOCK, 128), 1)
    top = k * BLOCK
    base = top // 128 * 128
    start, other = top - base, BLOCK - (top - base)
    held = (lane_of >= start) & (lane_of < start + BLOCK)
    tile = work[top : top + BLOCK, base : base + 128]
    tile = jnp.where(held, tile, jnp.where(lane_of - other == row_of, 1.0, 0.0))
    tile = eliminate(tile, start)
    inverse = jnp.where(held, pltpu.roll(tile, 64, 1), 0.0)
    solved = exact_dot(inverse, work[base : base + 128, :], NN)
    work[top : top + BLOCK, :] = solved
    if top + BLOCK < RANK:
        update = exact_dot(solved[:, :RANK], solved, TN)
        work[top + BLOCK :, :] = work[top + BLOCK :, :] - update[top + BLOCK :, :]


def factor_first_kernel(half_ref, got_ref, work):
    core = here()[0]
    work[at(core * BAND, BAND, BAND), :RANK] = half_ref[...]
    work[at((1 - core) * BAND, BAND, BAND), :RANK] = got_ref[...]
    rows = lax.broadcasted_iota(jnp.int32, (RANK, RANK), 0)
    lanes = lax.broadcasted_iota(jnp.int32, (RANK, RANK), 1)
    work[:, RANK:] = jnp.where(rows == lanes, 1.0, 0.0)
    factor_block(work, 0)
    factor_block(work, 1)


def factor_last_kernel(half_done, inverse_high, inverse_low, work):
    work[...] = half_done[...]
    factor_block(work, 2)
    factor_block(work, 3)
    inverse_high[...], inverse_low[...] = split(work[:, RANK:])


def basis_kernel(own_ref, other_ref, inverse_high, inverse_low, left_ref, high_ref, low_ref):
    inverse = inverse_high[...], inverse_low[...]
    for half, ref in ((here()[0], own_ref), (1 - here()[0], other_ref)):
        for k in range(HALF // 256):
            rows = at(half * HALF + k * 256, 256, 256)
            orthonormal = dot3(split(ref[:, k * 256 : (k + 1) * 256].T), inverse, NT)
            left_ref[rows, :] = (64.0 * orthonormal).astype(BF16)
            high_ref[rows, :], low_ref[rows, :] = split(orthonormal)


STEP = 256


def last_kernel(
    own_high, own_low, other_high, other_low, basis_high, basis_low, inverse_high, inverse_low,
    band, got, residual_ref, right_out, z_work, c_high, c_low, right_ref, held, sems
):
    core, kept = here()[0], kept_half(0, False)
    z_work[at(kept * BAND, BAND, BAND), :] = band[...]
    z_work[at((1 - kept) * BAND, BAND, BAND), :] = got[...]
    coefficient = dot3((inverse_high[...], inverse_low[...]), split(z_work[...]), NN)
    right_ref[...] = (coefficient * (1.0 / 64.0)).astype(BF16)
    right_copy = pltpu.make_async_copy(right_ref, right_out, sems.at[ROWS // STEP])
    right_copy.start()
    c_high[...], c_low[...] = split(coefficient)
    stacked = jnp.concatenate([c_high[...], c_high[...], c_low[...]], axis=0)
    copies = []
    for half, high, low in ((core, own_high, own_low), (1 - core, other_high, other_low)):
        for k in range(HALF // STEP):
            rows = at(half * HALF + k * STEP, STEP, STEP)
            here_rows = slice(k * STEP, (k + 1) * STEP)
            slot = held.at[len(copies)]
            first, second = basis_high[rows, :], basis_low[rows, :]
            product = dot(jnp.concatenate([first, second, first], axis=1), stacked, NN)
            weight = high[here_rows, :].astype(F32) + low[here_rows, :].astype(F32)
            slot[...] = (weight - product).astype(BF16)
            copies.append(
                pltpu.make_async_copy(slot, residual_ref.at[rows, :], sems.at[len(copies)])
            )
            copies[-1].start()
    for copy in copies + [right_copy]:
        copy.wait()


def last_product(parts_own, parts_other, basis, inverse, band, got):
    steps = ROWS // STEP
    return call(
        last_kernel, [((ROWS, COLS), BF16), ((RANK, COLS), BF16)],
        *parts_own, *parts_other, *basis, *inverse, band, got,
        out_specs=[HBM, HBM],
        scratch=[
            pltpu.VMEM((RANK, COLS), F32), pltpu.VMEM((RANK, COLS), BF16),
            pltpu.VMEM((RANK, COLS), BF16), pltpu.VMEM((RANK, COLS), BF16),
            pltpu.VMEM((steps, STEP, COLS), BF16), pltpu.SemaphoreType.DMA((steps + 1,)),
        ],
    )


def per_device(weight, sketch):
    send, *parts_other = first_product(True, weight, sketch)
    got = swap(send)
    keep, *parts_own = first_product(False, weight, sketch)
    own = sum_col(keep, got)
    other = swap(own)
    first = call(back_own_kernel, [((RANK, COLS), F32)], own, *parts_own)[0]
    bands = back_product(first, other, parts_other, True, lambda _: first)

    turned = ((RANK, COLS), BF16)
    send, *projected = call(
        second_send_kernel, [((HALF, RANK), F32), turned, turned], *bands, *parts_other
    )
    got = swap(send)
    keep = call(second_keep_kernel, [((HALF, RANK), F32)], *parts_own, *projected)[0]
    own = sum_col(keep, got)
    other = swap(own)
    first = call(back_own_kernel, [((RANK, COLS), F32)], own, *parts_own)[0]
    results = []
    side = gram_and_factor(own, other, results)
    next(side)
    bands = back_product(first, other, parts_other, False, side.send)
    next(side, None)
    inverse, left_adapter, basis = results[:2], results[2], results[3:]
    residual, right_adapter = last_product(
        parts_own, parts_other, basis, inverse, *bands
    )
    return residual, left_adapter, right_adapter


def solution(mesh):
    return jax.shard_map(
        per_device,
        mesh=mesh,
        in_specs=(P("row", "col"), P("col", None)),
        out_specs=(P("row", "col"), P("row", None), P(None, "col")),
        check_vma=False,
    )
```
